512 devices in a mesh: tm: 4 (over x), obs: 128 (over z, y, core).
Axes of the slice: x: 4, y: 4, z: 16, core: 2. Of those that a mesh axis runs over, the one named last changes fastest.
Arguments:
- control: float32 [3, 4, 256, 512], P(None, 'tm', 'obs'), may hold values from -6 to 6
- diffusivity: float32 [256, 512], P('obs'), may hold values from 0.2 to 1
- footprints: bfloat16 [512, 4, 128, 4096], P('obs', None, None, 'tm'), may hold values from -0.046875 to 0.046875
- tile_lists: int32 [512, 4], P('obs'), may hold values from 0 to 127, as said below
- tile_counts: int32 [512], P('obs'), may hold values from 1 to 4, as said below
- measured: float32 [3, 65536], P(None, 'obs'), may hold values from -4 to 4
- weight: float32 [3, 65536], P(None, 'obs'), may hold values from 0.5 to 4
Outputs:
- gradient: float32 [3, 4, 256, 512], P(None, 'tm', 'obs')
- residual: float32 [3, 65536], P(None, 'obs')
The draws below stay inside these ranges and needn't reach their ends.
Inputs may be any that keep to these rules, and one draw needn't show every extreme that they name: `tile_lists`: entry 0 of block b's list is tile b // 4, the tile of the block's own device; the 4 entries of one list are distinct; entries at positions tile_counts[b] or later are padding. `tile_counts`: the first block of every device has a full list.
All inputs are finite; a program needn't handle non-finite values.
Results may differ from the reference program's by a relative error of at most 0.002.
Values may be sent and summed in bfloat16 or wider, within the bound.
No kernel may reach another device: no remote copies, remote signals or barrier semaphores. Data moves between devices by JAX's collectives and lax.ppermute only.
A program may use at most 64 MiB of HBM per device.

```python
import math
import jax
import jax.numpy as jnp
from jax import lax

TR = 2
GW = 512
SB = 128
NB = 4
K = 4
ND = 2
TILES = 128
NR = 256
STEPS = 4
FOOT = 4096
BLOCKS = 512
SOUNDINGS = 65536


def draw_tile_lists(key, part):
    key = jax.random.fold_in(key, 11)
    block_keys = jax.random.split(key, BLOCKS)
    owners = (jnp.arange(BLOCKS, dtype=jnp.int32) // NB).astype(jnp.int32)

    def one_block(block_key, owner):
        others = jax.random.permutation(block_key, TILES - 1)[:K - 1].astype(jnp.int32)
        return jnp.concatenate([owner[None], (owner + 1 + others) % TILES]).astype(jnp.int32)
    return jax.vmap(one_block)(block_keys, owners)


def draw_tile_counts(key, part):
    key = jax.random.fold_in(key, 23)
    counts = jax.random.randint(key, (BLOCKS,), 1, K + 1).astype(jnp.int32)
    leading = jnp.arange(BLOCKS, dtype=jnp.int32) % NB == 0
    return jnp.where(leading, K, counts).astype(jnp.int32)


def levels(stream_key, shape, cuts, least, high):
    def one(axis_at, shards_of):
        draws = jax.random.uniform(jax.random.fold_in(jax.random.fold_in(stream_key, 6), axis_at), (shards_of,), jnp.float32, least / len(cuts), high / len(cuts))
        return jnp.repeat(jnp.exp(draws), shape[axis_at] // shards_of).reshape((-1,) + (1,) * (len(shape) - axis_at - 1))

    gain = one(*cuts[0])
    for cut in cuts[1:]:
        gain = gain * one(*cut)
    return gain


def bell_draw(own_key, shape, spread, reach, cuts=(), kind=jnp.bfloat16):
    factor_of = levels(own_key, shape, cuts, -0.22, 0.18) if cuts else 1.0
    result = jax.random.normal(own_key, shape, jnp.float32) * spread * factor_of
    return jnp.minimum(jnp.maximum(result, -reach), reach).astype(kind)


def setup_inputs(seed: int = 0) -> dict:
    streams_of = jax.random.split(jax.random.key(seed), 8)
    control = bell_draw(streams_of[0], (3, STEPS, NR, GW), 1.0, 6.0, ((1, 4), (2, 128)), jnp.float32)
    diffusivity = jnp.clip(0.2 + 0.8 * jax.random.uniform(streams_of[1], (NR, GW), jnp.float32) ** levels(streams_of[1], (NR, GW), ((0, 128),), -0.2, 0.2), 0.2, 1.0)
    footprints = bell_draw(streams_of[2], (BLOCKS, K, SB, FOOT), (K * FOOT) ** -0.5, 0.046875, ((0, 128), (3, 4)))
    tile_lists = draw_tile_lists(jax.random.fold_in(streams_of[7], 71), 0)
    tile_counts = draw_tile_counts(jax.random.fold_in(streams_of[7], 71), 0)
    measured = bell_draw(streams_of[5], (3, SOUNDINGS), 0.5, 4.0, ((1, 128),), jnp.float32)
    weight = jnp.clip(jnp.exp(math.log(4.0) - 2.0794415 * jax.random.uniform(streams_of[6], (3, SOUNDINGS), jnp.float32) ** levels(streams_of[6], (3, SOUNDINGS), ((1, 128),), -0.2, 0.2)), 0.5, 4.0)
    return {"control": control, "diffusivity": diffusivity, "footprints": footprints, "tile_lists": tile_lists, "tile_counts": tile_counts, "measured": measured, "weight": weight}


def diffuse_once(fields, conduct):
    middle = fields[:, 1:-1]
    conduct_mid = conduct[1:-1]
    zero_col = jnp.zeros_like(conduct_mid[:, :1])
    conduct_left = jnp.concatenate([zero_col, conduct_mid[:, :-1]], axis=1)
    conduct_right = jnp.concatenate([conduct_mid[:, 1:], zero_col], axis=1)
    zero_field = jnp.zeros_like(middle[:, :, :1])
    left_values = jnp.concatenate([zero_field, middle[:, :, :-1]], axis=2)
    right_values = jnp.concatenate([middle[:, :, 1:], zero_field], axis=2)
    return (middle
            + 0.0625 * (conduct_mid + conduct[:-2]) * (fields[:, :-2] - middle)
            + 0.0625 * (conduct_mid + conduct[2:]) * (fields[:, 2:] - middle)
            + 0.0625 * (conduct_mid + conduct_left) * (left_values - middle)
            + 0.0625 * (conduct_mid + conduct_right) * (right_values - middle))


def diffuse(fields, conduct):
    for repeat in range(ND):
        fields = diffuse_once(jnp.pad(fields, ((0, 0), (1, 1), (0, 0))), jnp.pad(conduct, ((1, 1), (0, 0))))
    return fields


def predict_block(pair):
    footprint, chosen = pair
    return jnp.einsum('kin,kcn->ci', footprint.astype(jnp.float32), chosen.astype(jnp.float32))


def adjoint_block(triple):
    footprint, misfit, usable = triple
    terms = jnp.einsum('kin,ci->kcn', footprint.astype(jnp.float32), misfit.astype(jnp.float32))
    return terms * usable.astype(jnp.float32)[:, None, None]


def reference(control, diffusivity, footprints, tile_lists, tile_counts, measured, weight):
    fields = control.reshape(3 * STEPS, NR, GW)
    flux_half = diffuse(fields, diffusivity).astype(jnp.bfloat16)
    panels = flux_half.reshape(3, STEPS, TILES, TR, GW).transpose(2, 0, 1, 3, 4).reshape(TILES, 3, FOOT)
    valid = jnp.arange(K, dtype=jnp.int32)[None, :] < tile_counts[:, None]
    chosen = panels[tile_lists]
    chosen = jnp.where(valid[:, :, None, None], chosen, jnp.zeros_like(chosen))
    predicted = lax.map(predict_block, (footprints, chosen))
    predicted = predicted.transpose(1, 0, 2).reshape(3, SOUNDINGS)
    residual = (predicted - measured) * weight
    residual_half = residual.astype(jnp.bfloat16)
    misfits = residual_half.reshape(3, BLOCKS, SB).transpose(1, 0, 2)
    adjoint = lax.map(adjoint_block, (footprints, misfits, valid))
    collected = jnp.zeros((TILES, 3, FOOT), jnp.float32).at[tile_lists.reshape(-1)].add(adjoint.reshape(BLOCKS * K, 3, FOOT))
    grid = collected.reshape(TILES, 3, STEPS, TR, GW).transpose(1, 2, 0, 3, 4).reshape(3 * STEPS, NR, GW)
    gradient = control + diffuse(grid, diffusivity).reshape(3, STEPS, NR, GW)
    return gradient, residual
```

```python
import jax
import jax.numpy as jnp
from jax import lax
from jax.sharding import Mesh, PartitionSpec as P

ZN, YN, CN = 16, 4, 2
OBS = ("z", "y", "c")


def sweep(fields, conduct):
    middle = fields[:, 1:-1]
    conduct_mid = conduct[1:-1]
    zero_col = jnp.zeros_like(conduct_mid[:, :1])
    conduct_left = jnp.concatenate([zero_col, conduct_mid[:, :-1]], axis=1)
    conduct_right = jnp.concatenate([conduct_mid[:, 1:], zero_col], axis=1)
    zero_field = jnp.zeros_like(middle[:, :, :1])
    left_values = jnp.concatenate([zero_field, middle[:, :, :-1]], axis=2)
    right_values = jnp.concatenate([middle[:, :, 1:], zero_field], axis=2)
    return (
        middle
        + 0.0625 * (conduct_mid + conduct[:-2]) * (fields[:, :-2] - middle)
        + 0.0625 * (conduct_mid + conduct[2:]) * (fields[:, 2:] - middle)
        + 0.0625 * (conduct_mid + conduct_left) * (left_values - middle)
        + 0.0625 * (conduct_mid + conduct_right) * (right_values - middle)
    )


def with_neighbours(own, core, tiles):
    mate = lax.ppermute(own, "c", [(0, 1), (1, 0)])
    pairs = [(i, i + 1) for i in range(1, tiles - 1, 2)]
    other = lax.ppermute(own, OBS, pairs + [(b, a) for a, b in pairs])
    before = jnp.where(core == 0, other, mate)
    after = jnp.where(core == 0, mate, other)
    return jnp.concatenate([before, own, after], axis=1)


def two_sweeps(fields, conduct, inside):
    return sweep(sweep(fields, conduct) * inside, conduct[1:-1])


def shards(control, diffusivity, footprints, tile_lists, tile_counts, measured, weight):
    tracers = control.shape[0]
    blocks, refs = tile_lists.shape
    tiles = ZN * YN * CN
    cells = control.shape[1] * control.shape[2] * control.shape[3]
    core = lax.axis_index("c")
    here = lax.axis_index(OBS)
    fields = control.reshape(tracers, 2, -1)

    ext = with_neighbours(jnp.concatenate([fields, diffusivity[None]], axis=0), core, tiles)
    conduct = ext[tracers]
    row = jnp.arange(4, dtype=jnp.int32)[:, None]
    inside = (((row > 0) | (here > 0)) & ((row < 3) | (here < tiles - 1))).astype(jnp.float32)
    flux_half = two_sweeps(ext[:tracers], conduct, inside).astype(jnp.bfloat16)

    own_panel = flux_half.reshape(1, tracers * cells)
    by_z = lax.all_to_all(jnp.broadcast_to(own_panel, (ZN, tracers * cells)), "z", 0, 0, tiled=True)
    by_y = lax.all_to_all(jnp.broadcast_to(by_z[None], (YN,) + by_z.shape), "y", 0, 0, tiled=True)
    panels = lax.all_gather(by_y.reshape(YN * ZN, tracers * cells), "c", axis=0, tiled=True)

    slot = jnp.arange(tiles, dtype=jnp.int32)
    owner = (slot % ZN) * (YN * CN) + (slot // ZN) % YN * CN + slot // (ZN * YN)
    valid = (jnp.arange(refs, dtype=jnp.int32)[None, :] < tile_counts[:, None]).reshape(-1)
    picks = (tile_lists.reshape(-1)[:, None] == owner[None, :]) & valid[:, None]
    chosen = jnp.dot(picks.astype(jnp.bfloat16), panels, preferred_element_type=jnp.float32)
    chosen = chosen.astype(jnp.bfloat16).reshape(blocks, refs, tracers, cells)
    part = jnp.einsum("bkin,bkcn->cbi", footprints, chosen, preferred_element_type=jnp.float32)
    predicted = lax.psum(part, "tm").reshape(tracers, -1)
    residual = (predicted - measured) * weight
    residual_half = residual.astype(jnp.bfloat16).reshape(tracers, blocks, -1)

    adjoint = jnp.einsum("bkin,cbi->bkcn", footprints, residual_half, preferred_element_type=jnp.float32)
    adjoint = adjoint.reshape(blocks * refs, tracers * cells)
    dense = jnp.dot(
        picks.astype(jnp.float32).T, adjoint, precision=lax.Precision.HIGHEST, preferred_element_type=jnp.float32
    )
    over_c = lax.all_to_all(dense.reshape(CN, YN * ZN, -1), "c", 0, 0, tiled=True).sum(axis=0)
    over_y = lax.all_to_all(over_c.reshape(YN, ZN, -1), "y", 0, 0, tiled=True).sum(axis=0)
    over_z = lax.all_to_all(over_y.astype(jnp.bfloat16), "z", 0, 0, tiled=True)
    total = over_z.astype(jnp.float32).sum(axis=0).reshape(fields.shape)

    spread = two_sweeps(with_neighbours(total, core, tiles), conduct, inside)
    return control + spread.reshape(control.shape), residual


def solution(mesh):
    fine = Mesh(mesh.devices.reshape(mesh.shape["tm"], ZN, YN, CN), ("tm",) + OBS)
    placed = (
        P(None, "tm", OBS, None),
        P(OBS, None),
        P(OBS, None, None, "tm"),
        P(OBS, None),
        P(OBS),
        P(None, OBS),
        P(None, OBS),
    )
    return jax.shard_map(
        shards,
        mesh=fine,
        in_specs=placed,
        out_specs=(P(None, "tm", OBS, None), P(None, OBS)),
        check_vma=False,
    )
```

```python
import jax
import jax.numpy as jnp
from jax import lax
from jax.experimental import pallas as pl
from jax.experimental.pallas import tpu as pltpu
from jax.sharding import Mesh, PartitionSpec as P

ZN, YN, CN = 16, 4, 2
OBS = ("z", "y", "c")
TILES = ZN * YN * CN
TRACERS, ROWS, WIDTH = 3, 2, 512
LANES = 128
CHUNKS = WIDTH // LANES
SUB = ROWS * CHUNKS
CELLS = ROWS * WIDTH
BLOCKS, REFS, SIGHTS = 4, 4, 128
ENTRIES = BLOCKS * REFS
PAY = TRACERS * LANES
F32, BF16 = jnp.float32, jnp.bfloat16


VMEM = pl.BlockSpec(memory_space=pltpu.VMEM)
SMEM = pl.BlockSpec(memory_space=pltpu.SMEM)


def call(body, out, ins, scratch=(), name=None):
    return pl.pallas_call(
        body,
        out_shape=out,
        in_specs=ins,
        out_specs=jax.tree.map(lambda _: VMEM, out),
        scratch_shapes=list(scratch),
        name=name,
    )


def shape(*dims, dtype=F32):
    return jax.ShapeDtypeStruct(dims, dtype)


def block(value, t):
    return value[:, t * LANES : (t + 1) * LANES]


def pack_kernel(control, diffusivity, lists, counts, out):
    def rows(read):
        return jnp.concatenate([read(s // CHUNKS, s % CHUNKS * LANES) for s in range(SUB)], axis=0)

    for t in range(TRACERS):
        out[:, t * LANES : (t + 1) * LANES] = rows(lambda r, at, t=t: control[t, 0, r : r + 1, at : at + LANES])
    out[:, TRACERS * LANES : 4 * LANES] = rows(lambda r, at: diffusivity[r : r + 1, at : at + LANES])
    lane = lax.broadcasted_iota(jnp.int32, (1, LANES), 1)
    ids = jnp.full((1, LANES), -1, jnp.int32)
    for b in range(BLOCKS):
        for k in range(REFS):
            ids = jnp.where((lane == b * REFS + k) & (k < counts[b]), lists[b, k], ids)
    out[:, 4 * LANES :] = jnp.broadcast_to(ids.astype(F32), (SUB, LANES))


def around(both, other, core, t):
    own = both[core, :, t * LANES : (t + 1) * LANES]
    mate = both[1 - core, :, t * LANES : (t + 1) * LANES]
    far = other[:, t * LANES : (t + 1) * LANES]
    first = core == 0
    return jnp.concatenate([jnp.where(first, far, mate), own, jnp.where(first, mate, far)], axis=0)


class Sweeps:
    def __init__(self, conduct, here):
        whole = conduct.shape
        self.rows = whole[0]
        sub = lax.broadcasted_iota(jnp.int32, whole, 0)
        self.lane = lax.broadcasted_iota(jnp.int32, whole, 1)
        self.chunk = sub % CHUNKS
        grid_row = sub // CHUNKS - ROWS
        self.inside = ((grid_row >= 0) | (here > 0)) & ((grid_row < ROWS) | (here < TILES - 1))
        self.factors = [0.0625 * (conduct + nb) for nb in self.neighbours(conduct)]

    def neighbours(self, v):
        n = self.rows
        up = pltpu.roll(v, CHUNKS, 0)
        down = pltpu.roll(v, n - CHUNKS, 0)
        left = pltpu.roll(v, 1, 1)
        left = jnp.where(self.lane == 0, jnp.where(self.chunk == 0, 0.0, pltpu.roll(left, 1, 0)), left)
        right = pltpu.roll(v, LANES - 1, 1)
        right = jnp.where(
            self.lane == LANES - 1, jnp.where(self.chunk == CHUNKS - 1, 0.0, pltpu.roll(right, n - 1, 0)), right
        )
        return up, down, left, right

    def once(self, v):
        total = v
        for factor, nb in zip(self.factors, self.neighbours(v)):
            total = total + factor * (nb - v)
        return total

    def twice(self, v):
        return self.once(jnp.where(self.inside, self.once(v), 0.0))[SUB : 2 * SUB]


def flux_kernel(both, other, out):
    core, here = lax.axis_index("c"), lax.axis_index(OBS)
    sweeps = Sweeps(around(both, other, core, TRACERS), here)
    half = jnp.concatenate([sweeps.twice(around(both, other, core, t)) for t in range(TRACERS)], axis=1).astype(BF16)
    for z in range(ZN):
        out[z] = half


def diagonal():
    row = lax.broadcasted_iota(jnp.int32, (SUB, CELLS), 0)
    lane = lax.broadcasted_iota(jnp.int32, (SUB, CELLS), 1)
    return row == lane // LANES


def predict_kernel(panels, footprints, lists, counts, out):
    match = diagonal()
    for b in range(BLOCKS):
        total = None
        for k in range(REFS):
            tile = lists[b, k]
            slot = tile % CN * (YN * ZN) + tile // CN % YN * ZN + tile // (CN * YN)
            panel = panels[slot].astype(F32)
            take = match & (k < counts[b])
            left = jnp.concatenate(
                [jnp.where(take, jnp.concatenate([block(panel, t)] * SUB, axis=1), 0.0) for t in range(TRACERS)], axis=0
            ).astype(BF16)
            term = lax.dot_general(left, footprints[b, k], (((1,), (1,)), ((), ())), preferred_element_type=F32)
            total = term if total is None else total + term
        for t in range(TRACERS):
            out[t : t + 1, b * SIGHTS : (b + 1) * SIGHTS] = jnp.sum(
                total[t * SUB : (t + 1) * SUB], axis=0, keepdims=True
            )


def adjoint_kernel(predicted, measured, weight, footprints, residual, out):
    misfit = (predicted[...] - measured[...]) * weight[...]
    residual[...] = misfit
    row = lax.broadcasted_iota(jnp.int32, (SUB, LANES), 0)
    for b in range(BLOCKS):
        own = misfit[:, b * SIGHTS : (b + 1) * SIGHTS]
        left = jnp.concatenate(
            [jnp.broadcast_to(own[t : t + 1], (SUB, SIGHTS)) for t in range(TRACERS)], axis=0
        ).astype(BF16)
        for k in range(REFS):
            full = jnp.dot(left, footprints[b, k], preferred_element_type=F32)
            for t in range(TRACERS):
                mine = full[t * SUB : (t + 1) * SUB]
                value = block(mine, 0)
                for q in range(1, SUB):
                    value = jnp.where(row == q, block(mine, q), value)
                out[b * REFS + k, :, t * LANES : (t + 1) * LANES] = value


def place_kernel(entries, ids, out):
    core = lax.axis_index("c")
    out[...] = jnp.zeros_like(out)
    for c in range(CN):
        for e in range(ENTRIES):
            tile = ids[c, e]

            @pl.when((tile >= 0) & (tile % CN == core))
            def _(tile=tile, at=c * ENTRIES + e):
                y, z = tile // CN % YN, tile // (CN * YN)
                out[y, z] = out[y, z] + entries[at]


def final_kernel(total_both, total_other, both, other, out):
    core, here = lax.axis_index("c"), lax.axis_index(OBS)
    sweeps = Sweeps(around(both, other, core, TRACERS), here)
    for t in range(TRACERS):
        value = both[core, :, t * LANES : (t + 1) * LANES] + sweeps.twice(around(total_both, total_other, core, t))
        for s in range(SUB):
            r, at = s // CHUNKS, s % CHUNKS * LANES
            out[t, 0, r : r + 1, at : at + LANES] = value[s : s + 1]


def neighbours(own):
    pairs = [(i, i + 1) for i in range(1, TILES - 1, 2)]
    other = lax.ppermute(own, OBS, pairs + [(b, a) for a, b in pairs])
    return lax.all_gather(own, "c"), other


def shards(control, diffusivity, footprints, tile_lists, tile_counts, measured, weight):
    own = call(pack_kernel, shape(SUB, 5 * LANES), [VMEM, VMEM, SMEM, SMEM], name="pack")(
        control, diffusivity, tile_lists, tile_counts
    )
    both, other = neighbours(own)
    ids = both[:, 0, 4 * LANES : 4 * LANES + ENTRIES].astype(jnp.int32)
    flux = call(flux_kernel, shape(ZN, SUB, PAY, dtype=BF16), [VMEM] * 2, name="flux")(both, other)

    by_z = lax.all_to_all(flux, "z", 0, 0, tiled=True)
    by_y = lax.all_to_all(jnp.broadcast_to(by_z[None], (YN,) + by_z.shape), "y", 0, 0, tiled=True)
    panels = lax.all_gather(by_y.reshape(YN * ZN, SUB, PAY), "c", axis=0, tiled=True)

    part = call(predict_kernel, shape(TRACERS, BLOCKS * SIGHTS), [VMEM, VMEM, SMEM, SMEM], name="predict")(
        panels, footprints, tile_lists, tile_counts
    )
    predicted = lax.psum(part, "tm")
    residual, entries = call(
        adjoint_kernel, (shape(TRACERS, BLOCKS * SIGHTS), shape(ENTRIES, SUB, PAY)), [VMEM] * 4, name="adjoint"
    )(predicted, measured, weight, footprints)

    chip = lax.all_gather(entries, "c", axis=0, tiled=True)
    dense = call(place_kernel, shape(YN, ZN, SUB, PAY), [VMEM, SMEM], name="place")(chip, ids)
    over_y = lax.all_to_all(dense, "y", 0, 0, tiled=True).sum(axis=0)
    total = lax.all_to_all(over_y, "z", 0, 0, tiled=True).sum(axis=0)

    total_both, total_other = neighbours(total)
    gradient = call(final_kernel, shape(*control.shape), [VMEM] * 4, name="final")(total_both, total_other, both, other)
    return gradient, residual


def solution(mesh):
    fine = Mesh(mesh.devices.reshape(mesh.shape["tm"], ZN, YN, CN), ("tm",) + OBS)
    placed = (
        P(None, "tm", OBS, None),
        P(OBS, None),
        P(OBS, None, None, "tm"),
        P(OBS, None),
        P(OBS),
        P(None, OBS),
        P(None, OBS),
    )
    return jax.shard_map(
        shards,
        mesh=fine,
        in_specs=placed,
        out_specs=(P(None, "tm", OBS, None), P(None, OBS)),
        check_vma=False,
    )
```

```python
import jax
import jax.numpy as jnp
from jax import lax
from jax.experimental import pallas as pl
from jax.experimental.pallas import tpu as pltpu
from jax.sharding import Mesh, PartitionSpec as P

ZN, YN, CN = 16, 4, 2
OBS = ("z", "y", "c")
TILES = ZN * YN * CN
TRACERS, ROWS, WIDTH = 3, 2, 512
LANES = 128
CHUNKS = WIDTH // LANES
SUB = ROWS * CHUNKS
CELLS = ROWS * WIDTH
BLOCKS, REFS, SIGHTS = 4, 4, 128
ENTRIES = BLOCKS * REFS
PAY = TRACERS * LANES
F32, BF16 = jnp.float32, jnp.bfloat16


VMEM = pl.BlockSpec(memory_space=pltpu.VMEM)
SMEM = pl.BlockSpec(memory_space=pltpu.SMEM)
MIB = 1 << 20


def call(body, out, ins, mib, scratch=(), name=None):
    return pl.pallas_call(
        body,
        out_shape=out,
        in_specs=ins,
        out_specs=jax.tree.map(lambda _: VMEM, out),
        scratch_shapes=list(scratch),
        compiler_params=pltpu.CompilerParams(vmem_limit_bytes=mib * MIB),
        name=name,
    )


def shape(*dims, dtype=F32):
    return jax.ShapeDtypeStruct(dims, dtype)


def block(value, t):
    return value[:, t * LANES : (t + 1) * LANES]


IDS, SEEN = 4, 5
PACK = 8 * LANES


def seen_row(which, t, b):
    at = (which * TRACERS + t) * BLOCKS + b
    return at % SUB, (SEEN + at // SUB) * LANES


def pack_kernel(control, diffusivity, measured, weight, lists, counts, out):
    def rows(read):
        return jnp.concatenate([read(s // CHUNKS, s % CHUNKS * LANES) for s in range(SUB)], axis=0)

    for t in range(TRACERS):
        out[:, t * LANES : (t + 1) * LANES] = rows(lambda r, at, t=t: control[t, 0, r : r + 1, at : at + LANES])
    out[:, TRACERS * LANES : 4 * LANES] = rows(lambda r, at: diffusivity[r : r + 1, at : at + LANES])
    lane = lax.broadcasted_iota(jnp.int32, (1, LANES), 1)
    ids = jnp.full((1, LANES), -1, jnp.int32)
    for b in range(BLOCKS):
        for k in range(REFS):
            ids = jnp.where((lane == b * REFS + k) & (k < counts[b]), lists[b, k], ids)
    out[:, IDS * LANES : SEEN * LANES] = jnp.broadcast_to(ids.astype(F32), (SUB, LANES))
    for which, ref in enumerate((measured, weight)):
        for t in range(TRACERS):
            for b in range(BLOCKS):
                r, at = seen_row(which, t, b)
                out[r : r + 1, at : at + LANES] = ref[t : t + 1, b * SIGHTS : (b + 1) * SIGHTS]


def around(both, other, core, t):
    own = both[core, :, t * LANES : (t + 1) * LANES]
    mate = both[1 - core, :, t * LANES : (t + 1) * LANES]
    far = other[:, t * LANES : (t + 1) * LANES]
    first = core == 0
    return jnp.concatenate([jnp.where(first, far, mate), own, jnp.where(first, mate, far)], axis=0)


class Sweeps:
    def __init__(self, conduct, here):
        whole = conduct.shape
        self.rows = whole[0]
        sub = lax.broadcasted_iota(jnp.int32, whole, 0)
        self.lane = lax.broadcasted_iota(jnp.int32, whole, 1)
        self.chunk = sub % CHUNKS
        grid_row = sub // CHUNKS - ROWS
        self.inside = ((grid_row >= 0) | (here > 0)) & ((grid_row < ROWS) | (here < TILES - 1))
        self.factors = [0.0625 * (conduct + nb) for nb in self.neighbours(conduct)]

    def neighbours(self, v):
        n = self.rows
        up = pltpu.roll(v, CHUNKS, 0)
        down = pltpu.roll(v, n - CHUNKS, 0)
        left = pltpu.roll(v, 1, 1)
        left = jnp.where(self.lane == 0, jnp.where(self.chunk == 0, 0.0, pltpu.roll(left, 1, 0)), left)
        right = pltpu.roll(v, LANES - 1, 1)
        right = jnp.where(
            self.lane == LANES - 1, jnp.where(self.chunk == CHUNKS - 1, 0.0, pltpu.roll(right, n - 1, 0)), right
        )
        return up, down, left, right

    def once(self, v):
        total = v
        for factor, nb in zip(self.factors, self.neighbours(v)):
            total = total + factor * (nb - v)
        return total

    def twice(self, v):
        return self.once(jnp.where(self.inside, self.once(v), 0.0))[SUB : 2 * SUB]


def flux_kernel(both, other, out):
    core, here = lax.axis_index("c"), lax.axis_index(OBS)
    sweeps = Sweeps(around(both, other, core, TRACERS), here)
    half = jnp.concatenate([sweeps.twice(around(both, other, core, t)) for t in range(TRACERS)], axis=1).astype(BF16)
    for z in range(ZN):
        out[z] = half


def diagonal():
    row = lax.broadcasted_iota(jnp.int32, (SUB, CELLS), 0)
    lane = lax.broadcasted_iota(jnp.int32, (SUB, CELLS), 1)
    return row == lane // LANES


def predict_kernel(panels, own, mate, ids, out, total):
    core = lax.axis_index("c")
    match = diagonal()
    for source, c in ((own, core), (mate, 1 - core)):
        for b in range(BLOCKS):
            total[...] = jnp.zeros_like(total)
            for k in range(REFS):
                tile = ids[c, b * REFS + k]

                @pl.when((tile >= 0) & (tile % CN == core))
                def _(tile=tile, source=source, b=b, k=k):
                    panel = panels[tile // CN % YN, tile // (CN * YN)].astype(F32)
                    left = jnp.concatenate(
                        [
                            jnp.where(match, jnp.concatenate([block(panel, t)] * SUB, axis=1), 0.0)
                            for t in range(TRACERS)
                        ],
                        axis=0,
                    ).astype(BF16)
                    total[...] += lax.dot_general(
                        left, source[b, k], (((1,), (1,)), ((), ())), preferred_element_type=F32
                    )

            for t in range(TRACERS):
                row = jnp.sum(total[t * SUB : (t + 1) * SUB], axis=0, keepdims=True)
                out[0, pl.ds(t * SUB + c * BLOCKS + b, 1), :] = row
    whole = out[0]
    for peer in range(1, out.shape[0]):
        out[peer] = whole


def adjoint_kernel(parts, both, own, mate, ids, residual, out, misfit):
    core = lax.axis_index("c")
    whole = parts[0]
    for peer in range(1, parts.shape[0]):
        whole = whole + parts[peer]

    def seen(which):
        rows = []
        for t in range(TRACERS):
            for c in range(CN):
                for b in range(BLOCKS):
                    r, at = seen_row(which, t, b)
                    rows.append(both[c, r : r + 1, at : at + LANES])
        return jnp.concatenate(rows, axis=0)

    misfit[...] = (whole - seen(0)) * seen(1)
    for t in range(TRACERS):
        for b in range(BLOCKS):
            residual[t : t + 1, b * SIGHTS : (b + 1) * SIGHTS] = misfit[pl.ds(t * SUB + core * BLOCKS + b, 1), :]
    out[...] = jnp.zeros_like(out)
    row = lax.broadcasted_iota(jnp.int32, (SUB, LANES), 0)
    for source, c in ((own, core), (mate, 1 - core)):
        for b in range(BLOCKS):
            left = jnp.concatenate(
                [
                    jnp.broadcast_to(misfit[pl.ds(t * SUB + c * BLOCKS + b, 1), :], (SUB, SIGHTS))
                    for t in range(TRACERS)
                ],
                axis=0,
            ).astype(BF16)
            for k in range(REFS):
                tile = ids[c, b * REFS + k]

                @pl.when((tile >= 0) & (tile % CN == core))
                def _(tile=tile, source=source, b=b, k=k, left=left):
                    full = jnp.dot(left, source[b, k], preferred_element_type=F32)
                    values = []
                    for t in range(TRACERS):
                        mine = full[t * SUB : (t + 1) * SUB]
                        value = block(mine, 0)
                        for q in range(1, SUB):
                            value = jnp.where(row == q, block(mine, q), value)
                        values.append(value)
                    y, z = tile // CN % YN, tile // (CN * YN)
                    out[y, z] = out[y, z] + jnp.concatenate(values, axis=1)


def final_kernel(total_both, total_other, both, other, out):
    core, here = lax.axis_index("c"), lax.axis_index(OBS)
    sweeps = Sweeps(around(both, other, core, TRACERS), here)
    for t in range(TRACERS):
        value = both[core, :, t * LANES : (t + 1) * LANES] + sweeps.twice(around(total_both, total_other, core, t))
        for s in range(SUB):
            r, at = s // CHUNKS, s % CHUNKS * LANES
            out[t, 0, r : r + 1, at : at + LANES] = value[s : s + 1]


def neighbours(own, width):
    pairs = [(i, i + 1) for i in range(1, TILES - 1, 2)]
    other = lax.ppermute(own[:, :width], OBS, pairs + [(b, a) for a, b in pairs])
    return lax.all_gather(own, "c"), other


def shards(control, diffusivity, footprints, tile_lists, tile_counts, measured, weight):
    own = call(pack_kernel, shape(SUB, PACK), [VMEM] * 4 + [SMEM] * 2, 1, name="pack")(
        control, diffusivity, measured, weight, tile_lists, tile_counts
    )
    both, other = neighbours(own, IDS * LANES)
    mate = lax.ppermute(footprints, "c", [(0, 1), (1, 0)])
    ids = both[:, 0, IDS * LANES : IDS * LANES + ENTRIES].astype(jnp.int32)
    flux = call(flux_kernel, shape(ZN, SUB, PAY, dtype=BF16), [VMEM] * 2, 2, name="flux")(both, other)

    by_z = lax.all_to_all(flux, "z", 0, 0, tiled=True)
    panels = lax.all_to_all(jnp.broadcast_to(by_z[None], (YN,) + by_z.shape), "y", 0, 0, tiled=True)

    peers = lax.axis_size("tm") * CN
    part = call(
        predict_kernel,
        shape(peers, TRACERS * SUB, LANES),
        [VMEM] * 3 + [SMEM],
        12,
        [pltpu.VMEM((TRACERS * SUB, LANES), F32)],
        name="predict",
    )(panels, footprints, mate, ids)
    parts = lax.all_to_all(part, ("tm", "c"), 0, 0, tiled=True)
    residual, dense = call(
        adjoint_kernel,
        (shape(TRACERS, BLOCKS * SIGHTS), shape(YN, ZN, SUB, PAY)),
        [VMEM] * 4 + [SMEM],
        12,
        [pltpu.VMEM((TRACERS * SUB, LANES), F32)],
        name="adjoint",
    )(parts, both, footprints, mate, ids)

    over_y = lax.all_to_all(dense, "y", 0, 0, tiled=True).sum(axis=0)
    total = lax.all_to_all(over_y, "z", 0, 0, tiled=True).sum(axis=0)

    total_both, total_other = neighbours(total, PAY)
    gradient = call(final_kernel, shape(*control.shape), [VMEM] * 4, 2, name="final")(
        total_both, total_other, both, other
    )
    return gradient, residual


def solution(mesh):
    fine = Mesh(mesh.devices.reshape(mesh.shape["tm"], ZN, YN, CN), ("tm",) + OBS)
    placed = (
        P(None, "tm", OBS, None),
        P(OBS, None),
        P(OBS, None, None, "tm"),
        P(OBS, None),
        P(OBS),
        P(None, OBS),
        P(None, OBS),
    )
    return jax.shard_map(
        shards,
        mesh=fine,
        in_specs=placed,
        out_specs=(P(None, "tm", OBS, None), P(None, OBS)),
        check_vma=False,
    )
```

```python
import jax
import jax.numpy as jnp
from jax import lax
from jax.experimental import pallas as pl
from jax.experimental.pallas import tpu as pltpu
from jax.sharding import Mesh, PartitionSpec as P

ZN, YN, CN = 16, 4, 2
OBS = ("z", "y", "c")
TILES = ZN * YN * CN
TRACERS, ROWS, WIDTH = 3, 2, 512
LANES = 128
CHUNKS = WIDTH // LANES
SUB = ROWS * CHUNKS
CELLS = ROWS * WIDTH
BLOCKS, REFS, SIGHTS = 4, 4, 128
ENTRIES = BLOCKS * REFS
PAY = TRACERS * LANES
F32, BF16 = jnp.float32, jnp.bfloat16


VMEM = pl.BlockSpec(memory_space=pltpu.VMEM)
SMEM = pl.BlockSpec(memory_space=pltpu.SMEM)
ANY = pl.BlockSpec(memory_space=pl.ANY)
MIB = 1 << 20


def call(body, out, ins, mib, scratch=(), name=None):
    return pl.pallas_call(
        body,
        out_shape=out,
        in_specs=ins,
        out_specs=jax.tree.map(lambda _: VMEM, out),
        scratch_shapes=list(scratch),
        compiler_params=pltpu.CompilerParams(vmem_limit_bytes=mib * MIB),
        name=name,
    )


def shape(*dims, dtype=F32):
    return jax.ShapeDtypeStruct(dims, dtype)


def block(value, t):
    return value[:, t * LANES : (t + 1) * LANES]


IDS, SEEN = 4, 5
PACK = 8 * LANES


def seen_row(which, t, b):
    at = (which * TRACERS + t) * BLOCKS + b
    return at % SUB, (SEEN + at // SUB) * LANES


def pack_kernel(*refs):
    sources, (lists, counts, out), targets, sem = refs[:4], refs[4:7], refs[7:11], refs[11]
    copies = [pltpu.make_async_copy(a, b, sem.at[i]) for i, (a, b) in enumerate(zip(sources, targets))]
    for copy in copies:
        copy.start()
    for copy in copies:
        copy.wait()
    control, diffusivity, measured, weight = targets

    def rows(read):
        return jnp.concatenate([read(s // CHUNKS, s % CHUNKS * LANES) for s in range(SUB)], axis=0)

    for t in range(TRACERS):
        out[:, t * LANES : (t + 1) * LANES] = rows(lambda r, at, t=t: control[t, 0, r : r + 1, at : at + LANES])
    out[:, TRACERS * LANES : 4 * LANES] = rows(lambda r, at: diffusivity[r : r + 1, at : at + LANES])
    lane = lax.broadcasted_iota(jnp.int32, (1, LANES), 1)
    ids = jnp.full((1, LANES), -1, jnp.int32)
    for b in range(BLOCKS):
        for k in range(REFS):
            ids = jnp.where((lane == b * REFS + k) & (k < counts[b]), lists[b, k], ids)
    out[:, IDS * LANES : SEEN * LANES] = jnp.broadcast_to(ids.astype(F32), (SUB, LANES))
    for which, ref in enumerate((measured, weight)):
        for t in range(TRACERS):
            for b in range(BLOCKS):
                r, at = seen_row(which, t, b)
                out[r : r + 1, at : at + LANES] = ref[t : t + 1, b * SIGHTS : (b + 1) * SIGHTS]


def around(both, other, core, t):
    own = both[core, :, t * LANES : (t + 1) * LANES]
    mate = both[1 - core, :, t * LANES : (t + 1) * LANES]
    far = other[:, t * LANES : (t + 1) * LANES]
    first = core == 0
    return jnp.concatenate([jnp.where(first, far, mate), own, jnp.where(first, mate, far)], axis=0)


class Sweeps:
    def __init__(self, conduct, here):
        whole = conduct.shape
        self.rows = whole[0]
        sub = lax.broadcasted_iota(jnp.int32, whole, 0)
        self.lane = lax.broadcasted_iota(jnp.int32, whole, 1)
        self.chunk = sub % CHUNKS
        grid_row = sub // CHUNKS - ROWS
        self.inside = ((grid_row >= 0) | (here > 0)) & ((grid_row < ROWS) | (here < TILES - 1))
        self.factors = [0.0625 * (conduct + nb) for nb in self.neighbours(conduct)]

    def neighbours(self, v):
        n = self.rows
        up = pltpu.roll(v, CHUNKS, 0)
        down = pltpu.roll(v, n - CHUNKS, 0)
        left = pltpu.roll(v, 1, 1)
        left = jnp.where(self.lane == 0, jnp.where(self.chunk == 0, 0.0, pltpu.roll(left, 1, 0)), left)
        right = pltpu.roll(v, LANES - 1, 1)
        right = jnp.where(
            self.lane == LANES - 1, jnp.where(self.chunk == CHUNKS - 1, 0.0, pltpu.roll(right, n - 1, 0)), right
        )
        return up, down, left, right

    def once(self, v):
        total = v
        for factor, nb in zip(self.factors, self.neighbours(v)):
            total = total + factor * (nb - v)
        return total

    def twice(self, v):
        return self.once(jnp.where(self.inside, self.once(v), 0.0))[SUB : 2 * SUB]


def flux_kernel(both, other, out):
    core, here = lax.axis_index("c"), lax.axis_index(OBS)
    sweeps = Sweeps(around(both, other, core, TRACERS), here)
    half = jnp.concatenate([sweeps.twice(around(both, other, core, t)) for t in range(TRACERS)], axis=1).astype(BF16)
    for z in range(ZN):
        out[z] = half


def diagonal():
    row = lax.broadcasted_iota(jnp.int32, (SUB, CELLS), 0)
    lane = lax.broadcasted_iota(jnp.int32, (SUB, CELLS), 1)
    return row == lane // LANES


def copies_kernel(source, out):
    for y in range(YN):
        out[y] = source[...]


STEP = 4


def start_active(own, mate, ids, held, order, sem, core):
    count = jnp.int32(0)
    for source, c in ((own, core), (mate, 1 - core)):
        for e in range(ENTRIES):
            tile = ids[c, e]
            active = (tile >= 0) & (tile % CN == core)
            order[count] = c * ENTRIES + e

            @pl.when(active)
            def _(source=source, e=e, at=count):
                pltpu.make_async_copy(source.at[e // REFS, e % REFS], held.at[at], sem.at[at]).start()

            count = count + active.astype(jnp.int32)
    return count


def over_active(count, own, ids, held, order, sem, work):
    def step(i, carry):
        found = []
        for u in range(STEP):
            at = i * STEP + u
            real = at < count

            @pl.when(real)
            def _(at=at):
                pltpu.make_async_copy(own.at[0, 0], held.at[at], sem.at[at]).wait()

            place = jnp.minimum(at, count - 1)
            entry = order[place]
            found.append((real, entry // REFS, ids[entry // ENTRIES, entry % ENTRIES], held.at[place]))
        work(found)
        return carry

    lax.fori_loop(0, (count + STEP - 1) // STEP, step, 0)


def predict_kernel(panels, own, mate, ids, out, held, order, sem, totals):
    core = lax.axis_index("c")
    count = start_active(own, mate, ids, held, order, sem, core)
    match = diagonal()
    totals[...] = jnp.zeros_like(totals)

    def work(found):
        terms = []
        for real, _, tile, footprint in found:
            panel = panels[tile // CN % YN, tile // (CN * YN)].astype(F32)
            panel = jnp.where(real, panel, 0.0)
            left = jnp.concatenate(
                [jnp.where(match, jnp.concatenate([block(panel, t)] * SUB, axis=1), 0.0) for t in range(TRACERS)],
                axis=0,
            ).astype(BF16)
            terms.append(
                lax.dot_general(left, footprint[...], (((1,), (1,)), ((), ())), preferred_element_type=F32)
            )
        for (_, b, _, _), term in zip(found, terms):
            totals[b] = totals[b] + term

    over_active(count, own, ids, held, order, sem, work)
    rows = [
        jnp.sum(totals[b, t * SUB : (t + 1) * SUB], axis=0, keepdims=True)
        for t in range(TRACERS)
        for b in range(CN * BLOCKS)
    ]
    whole = jnp.concatenate(rows, axis=0)
    for peer in range(out.shape[0]):
        out[peer] = whole


def adjoint_kernel(parts, both, own, mate, ids, residual, out, held, order, sem, lefts, sums):
    core = lax.axis_index("c")
    count = start_active(own, mate, ids, held, order, sem, core)
    whole = parts[0]
    for peer in range(1, parts.shape[0]):
        whole = whole + parts[peer]

    def seen(which):
        rows = []
        for t in range(TRACERS):
            for c in range(CN):
                for b in range(BLOCKS):
                    r, at = seen_row(which, t, b)
                    rows.append(both[c, r : r + 1, at : at + LANES])
        return jnp.concatenate(rows, axis=0)

    misfit = (whole - seen(0)) * seen(1)
    for t in range(TRACERS):
        for b in range(BLOCKS):
            first, second = (misfit[t * SUB + c * BLOCKS + b : t * SUB + c * BLOCKS + b + 1] for c in range(CN))
            residual[t : t + 1, b * SIGHTS : (b + 1) * SIGHTS] = jnp.where(core == 0, first, second)
    for b in range(CN * BLOCKS):
        lefts[b] = jnp.concatenate(
            [jnp.broadcast_to(misfit[t * SUB + b : t * SUB + b + 1], (SUB, SIGHTS)) for t in range(TRACERS)], axis=0
        )
    sums[...] = jnp.zeros_like(sums)
    row = lax.broadcasted_iota(jnp.int32, (SUB, LANES), 0)

    def work(found):
        values = []
        for real, b, _, footprint in found:
            full = jnp.dot(lefts[b].astype(BF16), footprint[...], preferred_element_type=F32)
            blocks = []
            for t in range(TRACERS):
                mine = full[t * SUB : (t + 1) * SUB]
                value = block(mine, 0)
                for q in range(1, SUB):
                    value = jnp.where(row == q, block(mine, q), value)
                blocks.append(jnp.where(real, value, 0.0))
            values.append(jnp.concatenate(blocks, axis=1))
        for (_, _, tile, _), value in zip(found, values):
            y, z = tile // CN % YN, tile // (CN * YN)
            sums[y, z] = sums[y, z] + value

    over_active(count, own, ids, held, order, sem, work)
    out[...] = sums[...].astype(BF16)


def final_kernel(total_both, total_other, both, other, out):
    core, here = lax.axis_index("c"), lax.axis_index(OBS)
    sweeps = Sweeps(around(both, other, core, TRACERS), here)
    for t in range(TRACERS):
        value = both[core, :, t * LANES : (t + 1) * LANES] + sweeps.twice(around(total_both, total_other, core, t))
        for s in range(SUB):
            r, at = s // CHUNKS, s % CHUNKS * LANES
            out[t, 0, r : r + 1, at : at + LANES] = value[s : s + 1]


def neighbours(own, width):
    pairs = [(i, i + 1) for i in range(1, TILES - 1, 2)]
    other = lax.ppermute(own[:, :width], OBS, pairs + [(b, a) for a, b in pairs])
    return lax.all_gather(own, "c"), other


def shards(control, diffusivity, footprints, tile_lists, tile_counts, measured, weight):
    given = (control, diffusivity, measured, weight)
    own = call(
        pack_kernel,
        shape(SUB, PACK),
        [ANY] * 4 + [SMEM] * 2,
        1,
        [pltpu.VMEM(a.shape, F32) for a in given] + [pltpu.SemaphoreType.DMA((4,))],
        name="pack",
    )(*given, tile_lists, tile_counts)
    both, other = neighbours(own, IDS * LANES)
    both, footprints = lax.optimization_barrier((both, footprints))
    mate = lax.ppermute(footprints, "c", [(0, 1), (1, 0)])
    ids = both[:, 0, IDS * LANES : IDS * LANES + ENTRIES].astype(jnp.int32)
    flux = call(flux_kernel, shape(ZN, SUB, PAY, dtype=BF16), [VMEM] * 2, 2, name="flux")(both, other)

    by_z = lax.all_to_all(flux, "z", 0, 0, tiled=True)
    copies = call(copies_kernel, shape(YN, *by_z.shape, dtype=BF16), [VMEM], 2, name="copies")(by_z)
    panels = lax.all_to_all(copies, "y", 0, 0, tiled=True)

    peers = lax.axis_size("tm") * CN
    active = [
        pltpu.VMEM((CN * ENTRIES, SIGHTS, CELLS), BF16),
        pltpu.SMEM((CN * ENTRIES + 1,), jnp.int32),
        pltpu.SemaphoreType.DMA((CN * ENTRIES,)),
        pltpu.VMEM((CN * BLOCKS, TRACERS * SUB, LANES), F32),
    ]
    part = call(
        predict_kernel, shape(peers, TRACERS * SUB, LANES), [VMEM, ANY, ANY, SMEM], 16, active, name="predict"
    )(panels, footprints, mate, ids)
    parts = lax.all_to_all(part, ("tm", "c"), 0, 0, tiled=True)
    residual, dense = call(
        adjoint_kernel,
        (shape(TRACERS, BLOCKS * SIGHTS), shape(YN, ZN, SUB, PAY, dtype=BF16)),
        [VMEM, VMEM, ANY, ANY, SMEM],
        16,
        active + [pltpu.VMEM((YN, ZN, SUB, PAY), F32)],
        name="adjoint",
    )(parts, both, footprints, mate, ids)

    over_y = lax.all_to_all(dense, "y", 0, 0, tiled=True).astype(F32).sum(axis=0)
    total = lax.all_to_all(over_y, "z", 0, 0, tiled=True).sum(axis=0)

    total_both, total_other = neighbours(total, PAY)
    gradient = call(final_kernel, shape(*control.shape), [VMEM] * 4, 2, name="final")(
        total_both, total_other, both, other
    )
    return gradient, residual


def solution(mesh):
    fine = Mesh(mesh.devices.reshape(mesh.shape["tm"], ZN, YN, CN), ("tm",) + OBS)
    placed = (
        P(None, "tm", OBS, None),
        P(OBS, None),
        P(OBS, None, None, "tm"),
        P(OBS, None),
        P(OBS),
        P(None, OBS),
        P(None, OBS),
    )
    return jax.shard_map(
        shards,
        mesh=fine,
        in_specs=placed,
        out_specs=(P(None, "tm", OBS, None), P(None, OBS)),
        check_vma=False,
    )
```

```python
import jax
import jax.numpy as jnp
from jax import lax
from jax.experimental import pallas as pl
from jax.experimental.pallas import tpu as pltpu
from jax.sharding import Mesh, PartitionSpec as P

ZN, YN, CN = 16, 4, 2
OBS = ("z", "y", "c")
TILES = ZN * YN * CN
TRACERS, ROWS, WIDTH = 3, 2, 512
LANES = 128
CHUNKS = WIDTH // LANES
SUB = ROWS * CHUNKS
CELLS = ROWS * WIDTH
BLOCKS, REFS, SIGHTS = 4, 4, 128
ENTRIES = BLOCKS * REFS
PAY = TRACERS * LANES
F32, BF16 = jnp.float32, jnp.bfloat16


VMEM = pl.BlockSpec(memory_space=pltpu.VMEM)
SMEM = pl.BlockSpec(memory_space=pltpu.SMEM)
HBM = pl.BlockSpec(memory_space=pltpu.HBM)
MIB = 1 << 20


def call(body, out, ins, mib, scratch=(), name=None):
    return pl.pallas_call(
        body,
        out_shape=out,
        in_specs=ins,
        out_specs=jax.tree.map(lambda _: VMEM, out),
        scratch_shapes=list(scratch),
        compiler_params=pltpu.CompilerParams(vmem_limit_bytes=mib * MIB),
        name=name,
    )


def in_hbm(array):
    return pltpu.with_memory_space_constraint(array, pltpu.HBM)


def shape(*dims, dtype=F32):
    return jax.ShapeDtypeStruct(dims, dtype)


def block(value, t):
    return value[:, t * LANES : (t + 1) * LANES]


IDS, SEEN = 4, 5
PACK = 8 * LANES


def seen_row(which, t, b):
    at = (which * TRACERS + t) * BLOCKS + b
    return at % SUB, (SEEN + at // SUB) * LANES


def pack_kernel(*refs):
    sources, (out, head), targets, sem = refs[:6], refs[6:8], refs[8:14], refs[14]
    copies = [pltpu.make_async_copy(a, b, sem.at[i]) for i, (a, b) in enumerate(zip(sources, targets))]
    for copy in copies:
        copy.start()
    for copy in copies:
        copy.wait()
    control, diffusivity, measured, weight, lists, counts = targets

    def rows(read):
        return jnp.concatenate([read(s // CHUNKS, s % CHUNKS * LANES) for s in range(SUB)], axis=0)

    for t in range(TRACERS):
        head[:, t * LANES : (t + 1) * LANES] = rows(lambda r, at, t=t: control[t, 0, r : r + 1, at : at + LANES])
    head[:, TRACERS * LANES :] = rows(lambda r, at: diffusivity[r : r + 1, at : at + LANES])
    out[:, : IDS * LANES] = head[...]
    lane = lax.broadcasted_iota(jnp.int32, (BLOCKS, REFS), 1)
    row = lax.broadcasted_iota(jnp.int32, (BLOCKS, REFS), 0)
    limit = jnp.zeros((BLOCKS, REFS), jnp.int32)
    for b in range(BLOCKS):
        limit = jnp.where(row == b, counts[0:1, b : b + 1], limit)
    out[:BLOCKS, IDS * LANES : IDS * LANES + REFS] = jnp.where(lane < limit, lists[...], -1).astype(F32)
    for which, ref in enumerate((measured, weight)):
        for t in range(TRACERS):
            for b in range(BLOCKS):
                r, at = seen_row(which, t, b)
                out[r : r + 1, at : at + LANES] = ref[t : t + 1, b * SIGHTS : (b + 1) * SIGHTS]


def around(both, other, core, t):
    own = both[core, :, t * LANES : (t + 1) * LANES]
    mate = both[1 - core, :, t * LANES : (t + 1) * LANES]
    far = other[:, t * LANES : (t + 1) * LANES]
    first = core == 0
    return jnp.concatenate([jnp.where(first, far, mate), own, jnp.where(first, mate, far)], axis=0)


class Sweeps:
    def __init__(self, conduct, here):
        whole = conduct.shape
        self.rows = whole[0]
        sub = lax.broadcasted_iota(jnp.int32, whole, 0)
        self.lane = lax.broadcasted_iota(jnp.int32, whole, 1)
        self.chunk = sub % CHUNKS
        grid_row = sub // CHUNKS - ROWS
        self.inside = ((grid_row >= 0) | (here > 0)) & ((grid_row < ROWS) | (here < TILES - 1))
        self.factors = [0.0625 * (conduct + nb) for nb in self.neighbours(conduct)]

    def neighbours(self, v):
        n = self.rows
        up = pltpu.roll(v, CHUNKS, 0)
        down = pltpu.roll(v, n - CHUNKS, 0)
        left = pltpu.roll(v, 1, 1)
        left = jnp.where(self.lane == 0, jnp.where(self.chunk == 0, 0.0, pltpu.roll(left, 1, 0)), left)
        right = pltpu.roll(v, LANES - 1, 1)
        right = jnp.where(
            self.lane == LANES - 1, jnp.where(self.chunk == CHUNKS - 1, 0.0, pltpu.roll(right, n - 1, 0)), right
        )
        return up, down, left, right

    def once(self, v):
        total = v
        for factor, nb in zip(self.factors, self.neighbours(v)):
            total = total + factor * (nb - v)
        return total

    def twice(self, v):
        return self.once(jnp.where(self.inside, self.once(v), 0.0))[SUB : 2 * SUB]


def flux_kernel(both, other, out, ids):
    for c in range(CN):
        ids[c] = both[c, :BLOCKS, IDS * LANES : SEEN * LANES].astype(jnp.int32)
    core, here = lax.axis_index("c"), lax.axis_index(OBS)
    sweeps = Sweeps(around(both, other, core, TRACERS), here)
    half = jnp.concatenate([sweeps.twice(around(both, other, core, t)) for t in range(TRACERS)], axis=1).astype(BF16)
    for z in range(ZN):
        out[z] = half


def diagonal():
    row = lax.broadcasted_iota(jnp.int32, (SUB, CELLS), 0)
    lane = lax.broadcasted_iota(jnp.int32, (SUB, CELLS), 1)
    return row == lane // LANES


def copies_kernel(source, out):
    for y in range(YN):
        out[y] = source[...]


STEP = 4


def list_active(ids, order, which, core, c, found=None):
    count = jnp.int32(0)
    for e in range(ENTRIES):
        tile = ids[c, e // REFS, e % REFS]
        active = (tile >= 0) & (tile % CN == core)
        order[which, count] = e
        if found is not None:
            pl.when(active)(lambda e=e: found(e))
        count = count + active.astype(jnp.int32)
    return count


def over_active(count, footprints, ids, order, which, c, work, ready=None):
    def step(i, carry):
        entries = []
        for u in range(STEP):
            at = i * STEP + u
            real = at < count
            e = order[which, jnp.maximum(jnp.minimum(at, count - 1), 0)]
            if ready is not None:
                pl.when(real)(lambda e=e: ready(e))
            b, k = e // REFS, e % REFS
            entries.append((real, c * BLOCKS + b, ids[c, b, k], footprints.at[b, k]))
        work(entries)
        return carry

    lax.fori_loop(0, (count + STEP - 1) // STEP, step, 0)


def predict_kernel(panels, own, mate, ids, out, held, order, sem, totals):
    core = lax.axis_index("c")

    def copy(e):
        b, k = e // REFS, e % REFS
        return pltpu.make_async_copy(own.at[b, k], held.at[b, k], sem.at[e])

    count = list_active(ids, order, 0, core, core, lambda e: copy(e).start())
    count_mate = list_active(ids, order, 1, core, 1 - core)
    match = diagonal()
    totals[...] = jnp.zeros_like(totals)

    def work(found):
        terms = []
        for real, _, tile, footprint in found:
            panel = panels[tile // CN % YN, tile // (CN * YN)].astype(F32)
            panel = jnp.where(real, panel, 0.0)
            left = jnp.concatenate(
                [jnp.where(match, jnp.concatenate([block(panel, t)] * SUB, axis=1), 0.0) for t in range(TRACERS)],
                axis=0,
            ).astype(BF16)
            terms.append(
                lax.dot_general(left, footprint[...], (((1,), (1,)), ((), ())), preferred_element_type=F32)
            )
        for (_, b, _, _), term in zip(found, terms):
            totals[b] = totals[b] + term

    over_active(count_mate, mate, ids, order, 1, 1 - core, work)
    over_active(count, held, ids, order, 0, core, work, lambda e: copy(e).wait())
    rows = [
        jnp.sum(totals[b, t * SUB : (t + 1) * SUB], axis=0, keepdims=True)
        for t in range(TRACERS)
        for b in range(CN * BLOCKS)
    ]
    whole = jnp.concatenate(rows, axis=0)
    for peer in range(out.shape[0]):
        out[peer] = whole


def adjoint_kernel(parts, both, held, mate, ids, residual, out, order, lefts, sums):
    core = lax.axis_index("c")
    count = list_active(ids, order, 0, core, core)
    count_mate = list_active(ids, order, 1, core, 1 - core)
    whole = parts[0]
    for peer in range(1, parts.shape[0]):
        whole = whole + parts[peer]

    def seen(which):
        rows = []
        for t in range(TRACERS):
            for c in range(CN):
                for b in range(BLOCKS):
                    r, at = seen_row(which, t, b)
                    rows.append(both[c, r : r + 1, at : at + LANES])
        return jnp.concatenate(rows, axis=0)

    misfit = (whole - seen(0)) * seen(1)
    for t in range(TRACERS):
        for b in range(BLOCKS):
            first, second = (misfit[t * SUB + c * BLOCKS + b : t * SUB + c * BLOCKS + b + 1] for c in range(CN))
            residual[t : t + 1, b * SIGHTS : (b + 1) * SIGHTS] = jnp.where(core == 0, first, second)
    for b in range(CN * BLOCKS):
        lefts[b] = jnp.concatenate(
            [jnp.broadcast_to(misfit[t * SUB + b : t * SUB + b + 1], (SUB, SIGHTS)) for t in range(TRACERS)], axis=0
        )
    sums[...] = jnp.zeros_like(sums)
    row = lax.broadcasted_iota(jnp.int32, (SUB, LANES), 0)

    def work(found):
        values = []
        for real, b, _, footprint in found:
            full = jnp.dot(lefts[b].astype(BF16), footprint[...], preferred_element_type=F32)
            blocks = []
            for t in range(TRACERS):
                mine = full[t * SUB : (t + 1) * SUB]
                value = block(mine, 0)
                for q in range(1, SUB):
                    value = jnp.where(row == q, block(mine, q), value)
                blocks.append(jnp.where(real, value, 0.0))
            values.append(jnp.concatenate(blocks, axis=1))
        for (_, _, tile, _), value in zip(found, values):
            y, z = tile // CN % YN, tile // (CN * YN)
            sums[y, z] = sums[y, z] + value

    over_active(count, held, ids, order, 0, core, work)
    over_active(count_mate, mate, ids, order, 1, 1 - core, work)
    out[...] = sums[...].astype(BF16)


LEVELS = 6
FINE = 256.0


def fold_y_kernel(parts, out):
    for z in range(ZN):
        value = parts[0, z].astype(F32)
        for y in range(1, YN):
            value = value + parts[y, z].astype(F32)
        high = value.astype(BF16)
        near = high.astype(F32)
        size = jnp.abs(near)
        part = (value - near) * (FINE / jnp.where(size == 0.0, 1.0, size))
        level = jnp.clip(jnp.floor((part + 1.0) * (LEVELS / 2)), 0.0, LEVELS - 1.0)
        code = block(level, 0) + LEVELS * block(level, 1) + LEVELS * LEVELS * block(level, 2)
        out[z, :, :PAY] = high
        out[z, :, PAY:] = code.astype(BF16)


def fold_z_kernel(parts, out):
    total = None
    for z in range(ZN):
        near = parts[z, :, :PAY].astype(F32)
        code = parts[z, :, PAY:].astype(F32)
        third = jnp.floor((code + 0.5) * (1.0 / (LEVELS * LEVELS)))
        code = code - LEVELS * LEVELS * third
        second = jnp.floor((code + 0.5) * (1.0 / LEVELS))
        level = jnp.concatenate([code - LEVELS * second, second, third], axis=1)
        part = (level + 0.5) * (2.0 / LEVELS) - 1.0
        value = near + jnp.abs(near) * (part * (1.0 / FINE))
        total = value if total is None else total + value
    out[...] = total


def final_kernel(total_both, total_other, both, other, out):
    core, here = lax.axis_index("c"), lax.axis_index(OBS)
    sweeps = Sweeps(around(both, other, core, TRACERS), here)
    for t in range(TRACERS):
        value = both[core, :, t * LANES : (t + 1) * LANES] + sweeps.twice(around(total_both, total_other, core, t))
        for s in range(SUB):
            r, at = s // CHUNKS, s % CHUNKS * LANES
            out[t, 0, r : r + 1, at : at + LANES] = value[s : s + 1]


def neighbours(own, head):
    pairs = [(i, i + 1) for i in range(1, TILES - 1, 2)]
    other = lax.ppermute(head, OBS, pairs + [(b, a) for a, b in pairs])
    return lax.all_gather(own, "c"), other


def shards(control, diffusivity, footprints, tile_lists, tile_counts, measured, weight):
    given = (control, diffusivity, measured, weight, tile_lists, tile_counts.reshape(1, BLOCKS))
    own, head = call(
        pack_kernel,
        (shape(SUB, PACK), shape(SUB, IDS * LANES)),
        [HBM] * len(given),
        1,
        [pltpu.VMEM(a.shape, a.dtype) for a in given] + [pltpu.SemaphoreType.DMA((len(given),))],
        name="pack",
    )(*map(in_hbm, given))
    both, other = neighbours(own, head)
    flux, ids = call(
        flux_kernel,
        (shape(ZN, SUB, PAY, dtype=BF16), shape(CN, BLOCKS, LANES, dtype=jnp.int32)),
        [VMEM] * 2,
        2,
        name="flux",
    )(both, other)

    by_z = lax.all_to_all(flux, "z", 0, 0, tiled=True)
    by_z, footprints = lax.optimization_barrier((by_z, footprints))
    mate = lax.ppermute(footprints, "c", [(0, 1), (1, 0)])
    copies = call(copies_kernel, shape(YN, *by_z.shape, dtype=BF16), [VMEM], 2, name="copies")(by_z)
    panels = lax.all_to_all(copies, "y", 0, 0, tiled=True)

    peers = lax.axis_size("tm") * CN
    part, held = call(
        predict_kernel,
        (shape(peers, TRACERS * SUB, LANES), pltpu.VMEM(footprints.shape, BF16)),
        [VMEM, HBM, VMEM, SMEM],
        16,
        [
            pltpu.SMEM((CN, ENTRIES + 1), jnp.int32),
            pltpu.SemaphoreType.DMA((ENTRIES,)),
            pltpu.VMEM((CN * BLOCKS, TRACERS * SUB, LANES), F32),
        ],
        name="predict",
    )(panels, in_hbm(footprints), mate, ids)
    parts = lax.all_to_all(part, ("tm", "c"), 0, 0, tiled=True)
    residual, dense = call(
        adjoint_kernel,
        (shape(TRACERS, BLOCKS * SIGHTS), shape(YN, ZN, SUB, PAY, dtype=BF16)),
        [VMEM] * 4 + [SMEM],
        16,
        [
            pltpu.SMEM((CN, ENTRIES + 1), jnp.int32),
            pltpu.VMEM((CN * BLOCKS, TRACERS * SUB, LANES), F32),
            pltpu.VMEM((YN, ZN, SUB, PAY), F32),
        ],
        name="adjoint",
    )(parts, both, held, mate, ids)

    over_y = lax.all_to_all(dense, "y", 0, 0, tiled=True)
    coded = call(fold_y_kernel, shape(ZN, SUB, PAY + LANES, dtype=BF16), [VMEM], 2, name="fold_y")(over_y)
    over_z = lax.all_to_all(coded, "z", 0, 0, tiled=True)
    total = call(fold_z_kernel, shape(SUB, PAY), [VMEM], 2, name="fold_z")(over_z)

    total_both, total_other = neighbours(total, total)
    gradient = call(final_kernel, shape(*control.shape), [VMEM] * 4, 2, name="final")(
        total_both, total_other, both, other
    )
    return gradient, residual


def solution(mesh):
    fine = Mesh(mesh.devices.reshape(mesh.shape["tm"], ZN, YN, CN), ("tm",) + OBS)
    placed = (
        P(None, "tm", OBS, None),
        P(OBS, None),
        P(OBS, None, None, "tm"),
        P(OBS, None),
        P(OBS),
        P(None, OBS),
        P(None, OBS),
    )
    return jax.shard_map(
        shards,
        mesh=fine,
        in_specs=placed,
        out_specs=(P(None, "tm", OBS, None), P(None, OBS)),
        check_vma=False,
    )
```

```python
import jax
import jax.numpy as jnp
from jax import lax
from jax.experimental import pallas as pl
from jax.experimental.pallas import tpu as pltpu
from jax.sharding import Mesh, PartitionSpec as P

ZN, YN, CN = 16, 4, 2
OBS = ("z", "y", "c")
TILES = ZN * YN * CN
TRACERS, ROWS, WIDTH = 3, 2, 512
LANES = 128
CHUNKS = WIDTH // LANES
SUB = ROWS * CHUNKS
CELLS = ROWS * WIDTH
BLOCKS, REFS, SIGHTS = 4, 4, 128
ENTRIES = BLOCKS * REFS
PAY = TRACERS * LANES
F32, BF16 = jnp.float32, jnp.bfloat16


VMEM = pl.BlockSpec(memory_space=pltpu.VMEM)
SMEM = pl.BlockSpec(memory_space=pltpu.SMEM)
HBM = pl.BlockSpec(memory_space=pltpu.HBM)
MIB = 1 << 20


def call(body, out, ins, mib, scratch=(), name=None):
    return pl.pallas_call(
        body,
        out_shape=out,
        in_specs=ins,
        out_specs=jax.tree.map(lambda o: SMEM if getattr(o, "memory_space", None) == pltpu.SMEM else VMEM, out),
        scratch_shapes=list(scratch),
        compiler_params=pltpu.CompilerParams(vmem_limit_bytes=mib * MIB),
        name=name,
    )


def in_hbm(array):
    return pltpu.with_memory_space_constraint(array, pltpu.HBM)


def shape(*dims, dtype=F32):
    return jax.ShapeDtypeStruct(dims, dtype)


def block(value, t):
    return value[:, t * LANES : (t + 1) * LANES]


IDS, SEEN = 4, 5
PACK = 8 * LANES


def seen_row(which, t, b):
    at = (which * TRACERS + t) * BLOCKS + b
    return at % SUB, (SEEN + at // SUB) * LANES


def pack_kernel(*refs):
    sources, (out, head), targets, sem = refs[:6], refs[6:8], refs[8:14], refs[14]
    copies = [pltpu.make_async_copy(a, b, sem.at[i]) for i, (a, b) in enumerate(zip(sources, targets))]
    for copy in copies:
        copy.start()
    for copy in copies:
        copy.wait()
    control, diffusivity, measured, weight, lists, counts = targets

    def rows(read):
        return jnp.concatenate([read(s // CHUNKS, s % CHUNKS * LANES) for s in range(SUB)], axis=0)

    for t in range(TRACERS):
        head[:, t * LANES : (t + 1) * LANES] = rows(lambda r, at, t=t: control[t, 0, r : r + 1, at : at + LANES])
    head[:, TRACERS * LANES :] = rows(lambda r, at: diffusivity[r : r + 1, at : at + LANES])
    out[:, : IDS * LANES] = head[...]
    lane = lax.broadcasted_iota(jnp.int32, (BLOCKS, REFS), 1)
    row = lax.broadcasted_iota(jnp.int32, (BLOCKS, REFS), 0)
    limit = jnp.zeros((BLOCKS, REFS), jnp.int32)
    for b in range(BLOCKS):
        limit = jnp.where(row == b, counts[0:1, b : b + 1], limit)
    out[:BLOCKS, IDS * LANES : IDS * LANES + REFS] = jnp.where(lane < limit, lists[...], -1).astype(F32)
    for which, ref in enumerate((measured, weight)):
        for t in range(TRACERS):
            for b in range(BLOCKS):
                r, at = seen_row(which, t, b)
                out[r : r + 1, at : at + LANES] = ref[t : t + 1, b * SIGHTS : (b + 1) * SIGHTS]


def around(both, other, core, t):
    own = both[core, :, t * LANES : (t + 1) * LANES]
    mate = both[1 - core, :, t * LANES : (t + 1) * LANES]
    far = other[:, t * LANES : (t + 1) * LANES]
    first = core == 0
    return jnp.concatenate([jnp.where(first, far, mate), own, jnp.where(first, mate, far)], axis=0)


class Sweeps:
    def __init__(self, conduct, here):
        whole = conduct.shape
        self.rows = whole[0]
        sub = lax.broadcasted_iota(jnp.int32, whole, 0)
        self.lane = lax.broadcasted_iota(jnp.int32, whole, 1)
        self.chunk = sub % CHUNKS
        grid_row = sub // CHUNKS - ROWS
        self.inside = ((grid_row >= 0) | (here > 0)) & ((grid_row < ROWS) | (here < TILES - 1))
        self.factors = [0.0625 * (conduct + nb) for nb in self.neighbours(conduct)]

    def neighbours(self, v):
        n = self.rows
        up = pltpu.roll(v, CHUNKS, 0)
        down = pltpu.roll(v, n - CHUNKS, 0)
        left = pltpu.roll(v, 1, 1)
        left = jnp.where(self.lane == 0, jnp.where(self.chunk == 0, 0.0, pltpu.roll(left, 1, 0)), left)
        right = pltpu.roll(v, LANES - 1, 1)
        right = jnp.where(
            self.lane == LANES - 1, jnp.where(self.chunk == CHUNKS - 1, 0.0, pltpu.roll(right, n - 1, 0)), right
        )
        return up, down, left, right

    def once(self, v):
        total = v
        for factor, nb in zip(self.factors, self.neighbours(v)):
            total = total + factor * (nb - v)
        return total

    def twice(self, v):
        return self.once(jnp.where(self.inside, self.once(v), 0.0))[SUB : 2 * SUB]


def flux_kernel(both, other, out, ids):
    for c in range(CN):
        ids[c] = both[c, :BLOCKS, IDS * LANES : SEEN * LANES].astype(jnp.int32)
    core, here = lax.axis_index("c"), lax.axis_index(OBS)
    sweeps = Sweeps(around(both, other, core, TRACERS), here)
    half = jnp.concatenate([sweeps.twice(around(both, other, core, t)) for t in range(TRACERS)], axis=1).astype(BF16)
    for z in range(ZN):
        out[z] = half


def diagonal():
    row = lax.broadcasted_iota(jnp.int32, (SUB, CELLS), 0)
    lane = lax.broadcasted_iota(jnp.int32, (SUB, CELLS), 1)
    return row == lane // LANES


def copies_kernel(source, listed, out, ids, sem):
    copy = pltpu.make_async_copy(listed, ids, sem)
    copy.start()
    for y in range(YN):
        out[y] = source[...]
    copy.wait()


STEP = 4


def list_active(ids, order, which, core, c, found=None):
    count = jnp.int32(0)
    for e in range(ENTRIES):
        tile = ids[c, e // REFS, e % REFS]
        active = (tile >= 0) & (tile % CN == core)
        order[which, count] = e
        if found is not None:
            pl.when(active)(lambda e=e: found(e))
        count = count + active.astype(jnp.int32)
    return count


def over_active(count, footprints, ids, order, which, c, work, ready=None):
    def step(i, carry):
        entries = []
        for u in range(STEP):
            at = i * STEP + u
            real = at < count
            e = order[which, jnp.maximum(jnp.minimum(at, count - 1), 0)]
            if ready is not None:
                pl.when(real)(lambda e=e: ready(e))
            b, k = e // REFS, e % REFS
            entries.append((real, c * BLOCKS + b, ids[c, b, k], footprints.at[b, k]))
        work(entries)
        return carry

    lax.fori_loop(0, (count + STEP - 1) // STEP, step, 0)


def predict_kernel(panels, own, mate, ids, out, held, order, sem, totals):
    core = lax.axis_index("c")

    def copy(e):
        b, k = e // REFS, e % REFS
        return pltpu.make_async_copy(own.at[b, k], held.at[b, k], sem.at[e])

    count = list_active(ids, order, 0, core, core, lambda e: copy(e).start())
    count_mate = list_active(ids, order, 1, core, 1 - core)
    match = diagonal()
    totals[...] = jnp.zeros_like(totals)

    def work(found):
        terms = []
        for real, _, tile, footprint in found:
            panel = panels[tile // CN % YN, tile // (CN * YN)].astype(F32)
            panel = jnp.where(real, panel, 0.0)
            left = jnp.concatenate(
                [jnp.where(match, jnp.concatenate([block(panel, t)] * SUB, axis=1), 0.0) for t in range(TRACERS)],
                axis=0,
            ).astype(BF16)
            terms.append(
                lax.dot_general(left, footprint[...], (((1,), (1,)), ((), ())), preferred_element_type=F32)
            )
        for (_, b, _, _), term in zip(found, terms):
            totals[b] = totals[b] + term

    over_active(count_mate, mate, ids, order, 1, 1 - core, work)
    over_active(count, held, ids, order, 0, core, work, lambda e: copy(e).wait())
    rows = [
        jnp.sum(totals[b, t * SUB : (t + 1) * SUB], axis=0, keepdims=True)
        for t in range(TRACERS)
        for b in range(CN * BLOCKS)
    ]
    whole = jnp.concatenate(rows, axis=0)
    for peer in range(out.shape[0]):
        out[peer] = whole


def adjoint_kernel(parts, both, held, mate, ids, misfits, out, order, lefts, sums):
    core = lax.axis_index("c")
    count = list_active(ids, order, 0, core, core)
    count_mate = list_active(ids, order, 1, core, 1 - core)
    whole = parts[0]
    for peer in range(1, parts.shape[0]):
        whole = whole + parts[peer]

    def seen(which):
        rows = []
        for t in range(TRACERS):
            for c in range(CN):
                for b in range(BLOCKS):
                    r, at = seen_row(which, t, b)
                    rows.append(both[c, r : r + 1, at : at + LANES])
        return jnp.concatenate(rows, axis=0)

    misfit = (whole - seen(0)) * seen(1)
    misfits[...] = misfit
    for b in range(CN * BLOCKS):
        lefts[b] = jnp.concatenate(
            [jnp.broadcast_to(misfit[t * SUB + b : t * SUB + b + 1], (SUB, SIGHTS)) for t in range(TRACERS)], axis=0
        )
    sums[...] = jnp.zeros_like(sums)
    row = lax.broadcasted_iota(jnp.int32, (SUB, LANES), 0)

    def work(found):
        values = []
        for real, b, _, footprint in found:
            full = jnp.dot(lefts[b].astype(BF16), footprint[...], preferred_element_type=F32)
            blocks = []
            for t in range(TRACERS):
                mine = full[t * SUB : (t + 1) * SUB]
                value = block(mine, 0)
                for q in range(1, SUB):
                    value = jnp.where(row == q, block(mine, q), value)
                blocks.append(jnp.where(real, value, 0.0))
            values.append(jnp.concatenate(blocks, axis=1))
        for (_, _, tile, _), value in zip(found, values):
            y, z = tile // CN % YN, tile // (CN * YN)
            sums[y, z] = sums[y, z] + value

    over_active(count, held, ids, order, 0, core, work)
    over_active(count_mate, mate, ids, order, 1, 1 - core, work)
    out[...] = sums[...].astype(BF16)


LEVELS = 6
FINE = 256.0


def fold_y_kernel(parts, out):
    for z in range(ZN):
        value = parts[0, z].astype(F32)
        for y in range(1, YN):
            value = value + parts[y, z].astype(F32)
        wide = value * 65537.0
        near = wide - (wide - value)
        size = jnp.abs(near)
        part = (value - near) * (FINE / jnp.where(size == 0.0, 1.0, size))
        level = jnp.clip(jnp.floor((part + 1.0) * (LEVELS / 2)), 0.0, LEVELS - 1.0)
        code = block(level, 0) + LEVELS * block(level, 1) + LEVELS * LEVELS * block(level, 2)
        out[z, :, :PAY] = near.astype(BF16)
        out[z, :, PAY:] = code.astype(BF16)


def fold_z_kernel(parts, out):
    total = None
    for z in range(ZN):
        near = parts[z, :, :PAY].astype(F32)
        code = parts[z, :, PAY:].astype(F32)
        third = jnp.floor((code + 0.5) * (1.0 / (LEVELS * LEVELS)))
        code = code - LEVELS * LEVELS * third
        second = jnp.floor((code + 0.5) * (1.0 / LEVELS))
        level = jnp.concatenate([code - LEVELS * second, second, third], axis=1)
        part = (level + 0.5) * (2.0 / LEVELS) - 1.0
        value = near + jnp.abs(near) * (part * (1.0 / FINE))
        total = value if total is None else total + value
    out[...] = total


def final_kernel(total_both, total_other, both, other, misfits, out, residual):
    core, here = lax.axis_index("c"), lax.axis_index(OBS)
    for t in range(TRACERS):
        for b in range(BLOCKS):
            first, second = (misfits[at : at + 1] for at in (t * SUB + b, t * SUB + BLOCKS + b))
            residual[t : t + 1, b * SIGHTS : (b + 1) * SIGHTS] = jnp.where(core == 0, first, second)
    sweeps = Sweeps(around(both, other, core, TRACERS), here)
    for t in range(TRACERS):
        value = both[core, :, t * LANES : (t + 1) * LANES] + sweeps.twice(around(total_both, total_other, core, t))
        for s in range(SUB):
            r, at = s // CHUNKS, s % CHUNKS * LANES
            out[t, 0, r : r + 1, at : at + LANES] = value[s : s + 1]


def neighbours(own, head):
    pairs = [(i, i + 1) for i in range(1, TILES - 1, 2)]
    other = lax.ppermute(head, OBS, pairs + [(b, a) for a, b in pairs])
    return lax.all_gather(own, "c"), other


def run_predict(panels, footprints, mate, ids, peers):
    return call(
        predict_kernel,
        (shape(peers, TRACERS * SUB, LANES), pltpu.VMEM(footprints.shape, BF16)),
        [VMEM, HBM, VMEM, SMEM],
        16,
        [
            pltpu.SMEM((CN, ENTRIES + 1), jnp.int32),
            pltpu.SemaphoreType.DMA((ENTRIES,)),
            pltpu.VMEM((CN * BLOCKS, TRACERS * SUB, LANES), F32),
        ],
        name="predict",
    )(panels, in_hbm(footprints), mate, ids)


def run_adjoint(parts, both, held, mate, ids):
    return call(
        adjoint_kernel,
        (shape(TRACERS * SUB, SIGHTS), shape(YN, ZN, SUB, PAY, dtype=BF16)),
        [VMEM] * 4 + [SMEM],
        16,
        [
            pltpu.SMEM((CN, ENTRIES + 1), jnp.int32),
            pltpu.VMEM((CN * BLOCKS, TRACERS * SUB, LANES), F32),
            pltpu.VMEM((YN, ZN, SUB, PAY), F32),
        ],
        name="adjoint",
    )(parts, both, held, mate, ids)


def shards(control, diffusivity, footprints, tile_lists, tile_counts, measured, weight):
    given = (control, diffusivity, measured, weight, tile_lists, tile_counts.reshape(1, BLOCKS))
    own, head = call(
        pack_kernel,
        (shape(SUB, PACK), shape(SUB, IDS * LANES)),
        [HBM] * len(given),
        1,
        [pltpu.VMEM(a.shape, a.dtype) for a in given] + [pltpu.SemaphoreType.DMA((len(given),))],
        name="pack",
    )(*map(in_hbm, given))
    both, other = neighbours(own, head)
    flux, listed = call(
        flux_kernel,
        (shape(ZN, SUB, PAY, dtype=BF16), shape(CN, BLOCKS, LANES, dtype=jnp.int32)),
        [VMEM] * 2,
        2,
        name="flux",
    )(both, other)

    by_z = lax.all_to_all(flux, "z", 0, 0, tiled=True)
    by_z, footprints = lax.optimization_barrier((by_z, footprints))
    mate = lax.ppermute(footprints, "c", [(0, 1), (1, 0)])
    copies, ids = call(
        copies_kernel,
        (shape(YN, *by_z.shape, dtype=BF16), pltpu.SMEM(listed.shape, jnp.int32)),
        [VMEM] * 2,
        2,
        [pltpu.SemaphoreType.DMA],
        name="copies",
    )(by_z, listed)
    panels = lax.all_to_all(copies, "y", 0, 0, tiled=True)

    part, held = run_predict(panels, footprints, mate, ids, lax.axis_size("tm") * CN)
    parts = lax.all_to_all(part, ("tm", "c"), 0, 0, tiled=True)
    misfits, dense = run_adjoint(parts, both, held, mate, ids)

    over_y = lax.all_to_all(dense, "y", 0, 0, tiled=True)
    coded = call(fold_y_kernel, shape(ZN, SUB, PAY + LANES, dtype=BF16), [VMEM], 2, name="fold_y")(over_y)
    over_z = lax.all_to_all(coded, "z", 0, 0, tiled=True)
    total = call(fold_z_kernel, shape(SUB, PAY), [VMEM], 2, name="fold_z")(over_z)

    total_both, total_other = neighbours(total, total)
    return call(
        final_kernel,
        (shape(*control.shape), shape(TRACERS, BLOCKS * SIGHTS)),
        [VMEM] * 5,
        2,
        name="final",
    )(total_both, total_other, both, other, misfits)


def solution(mesh):
    fine = Mesh(mesh.devices.reshape(mesh.shape["tm"], ZN, YN, CN), ("tm",) + OBS)
    placed = (
        P(None, "tm", OBS, None),
        P(OBS, None),
        P(OBS, None, None, "tm"),
        P(OBS, None),
        P(OBS),
        P(None, OBS),
        P(None, OBS),
    )
    return jax.shard_map(
        shards,
        mesh=fine,
        in_specs=placed,
        out_specs=(P(None, "tm", OBS, None), P(None, OBS)),
        check_vma=False,
    )
```

```python
import jax
import jax.numpy as jnp
from jax import lax
from jax.experimental import pallas as pl
from jax.experimental.pallas import tpu as pltpu
from jax.sharding import Mesh, PartitionSpec as P

ZN, YN, CN = 16, 4, 2
OBS = ("z", "y", "c")
TILES = ZN * YN * CN
TRACERS, ROWS, WIDTH = 3, 2, 512
LANES = 128
CHUNKS = WIDTH // LANES
SUB = ROWS * CHUNKS
CELLS = ROWS * WIDTH
BLOCKS, REFS, SIGHTS = 4, 4, 128
ENTRIES = BLOCKS * REFS
PAY = TRACERS * LANES
F32, BF16 = jnp.float32, jnp.bfloat16


VMEM = pl.BlockSpec(memory_space=pltpu.VMEM)
SMEM = pl.BlockSpec(memory_space=pltpu.SMEM)
HBM = pl.BlockSpec(memory_space=pltpu.HBM)
MIB = 1 << 20


def call(body, out, ins, mib, scratch=(), name=None):
    return pl.pallas_call(
        body,
        out_shape=out,
        in_specs=ins,
        out_specs=jax.tree.map(lambda o: SMEM if getattr(o, "memory_space", None) == pltpu.SMEM else VMEM, out),
        scratch_shapes=list(scratch),
        compiler_params=pltpu.CompilerParams(vmem_limit_bytes=mib * MIB),
        name=name,
    )


def in_hbm(array):
    return pltpu.with_memory_space_constraint(array, pltpu.HBM)


def shape(*dims, dtype=F32):
    return jax.ShapeDtypeStruct(dims, dtype)


def block(value, t):
    return value[:, t * LANES : (t + 1) * LANES]


IDS, SEEN = 4, 5
PACK = 8 * LANES


def seen_row(which, t, b):
    at = (which * TRACERS + t) * BLOCKS + b
    return at % SUB, (SEEN + at // SUB) * LANES


def pack_kernel(*refs):
    sources, (out, head), targets, sem = refs[:6], refs[6:8], refs[8:14], refs[14]
    copies = [pltpu.make_async_copy(a, b, sem.at[i]) for i, (a, b) in enumerate(zip(sources, targets))]
    for copy in copies:
        copy.start()
    for copy in copies:
        copy.wait()
    control, diffusivity, measured, weight, lists, counts = targets

    def rows(read):
        return jnp.concatenate([read(s // CHUNKS, s % CHUNKS * LANES) for s in range(SUB)], axis=0)

    for t in range(TRACERS):
        head[:, t * LANES : (t + 1) * LANES] = rows(lambda r, at, t=t: control[t, 0, r : r + 1, at : at + LANES])
    head[:, TRACERS * LANES :] = rows(lambda r, at: diffusivity[r : r + 1, at : at + LANES])
    out[:, : IDS * LANES] = head[...]
    lane = lax.broadcasted_iota(jnp.int32, (BLOCKS, REFS), 1)
    row = lax.broadcasted_iota(jnp.int32, (BLOCKS, REFS), 0)
    limit = jnp.zeros((BLOCKS, REFS), jnp.int32)
    for b in range(BLOCKS):
        limit = jnp.where(row == b, counts[0:1, b : b + 1], limit)
    out[:BLOCKS, IDS * LANES : IDS * LANES + REFS] = jnp.where(lane < limit, lists[...], -1).astype(F32)
    for which, ref in enumerate((measured, weight)):
        for t in range(TRACERS):
            for b in range(BLOCKS):
                r, at = seen_row(which, t, b)
                out[r : r + 1, at : at + LANES] = ref[t : t + 1, b * SIGHTS : (b + 1) * SIGHTS]


def around(both, other, core, t):
    own = both[core, :, t * LANES : (t + 1) * LANES]
    mate = both[1 - core, :, t * LANES : (t + 1) * LANES]
    far = other[:, t * LANES : (t + 1) * LANES]
    first = core == 0
    return jnp.concatenate([jnp.where(first, far, mate), own, jnp.where(first, mate, far)], axis=0)


class Sweeps:
    def __init__(self, conduct, here):
        whole = conduct.shape
        self.rows = whole[0]
        sub = lax.broadcasted_iota(jnp.int32, whole, 0)
        self.lane = lax.broadcasted_iota(jnp.int32, whole, 1)
        self.chunk = sub % CHUNKS
        grid_row = sub // CHUNKS - ROWS
        self.inside = ((grid_row >= 0) | (here > 0)) & ((grid_row < ROWS) | (here < TILES - 1))
        self.factors = [0.0625 * (conduct + nb) for nb in self.neighbours(conduct)]

    def neighbours(self, v):
        n = self.rows
        up = pltpu.roll(v, CHUNKS, 0)
        down = pltpu.roll(v, n - CHUNKS, 0)
        left = pltpu.roll(v, 1, 1)
        left = jnp.where(self.lane == 0, jnp.where(self.chunk == 0, 0.0, pltpu.roll(left, 1, 0)), left)
        right = pltpu.roll(v, LANES - 1, 1)
        right = jnp.where(
            self.lane == LANES - 1, jnp.where(self.chunk == CHUNKS - 1, 0.0, pltpu.roll(right, n - 1, 0)), right
        )
        return up, down, left, right

    def once(self, v):
        total = v
        for factor, nb in zip(self.factors, self.neighbours(v)):
            total = total + factor * (nb - v)
        return total

    def twice(self, v):
        return self.once(jnp.where(self.inside, self.once(v), 0.0))[SUB : 2 * SUB]


def flux_kernel(both, other, out, ids):
    for c in range(CN):
        ids[c] = both[c, :BLOCKS, IDS * LANES : SEEN * LANES].astype(jnp.int32)
    core, here = lax.axis_index("c"), lax.axis_index(OBS)
    sweeps = Sweeps(around(both, other, core, TRACERS), here)
    half = jnp.concatenate([sweeps.twice(around(both, other, core, t)) for t in range(TRACERS)], axis=1).astype(BF16)
    for z in range(ZN):
        out[z] = half


def diagonal():
    row = lax.broadcasted_iota(jnp.int32, (SUB, CELLS), 0)
    lane = lax.broadcasted_iota(jnp.int32, (SUB, CELLS), 1)
    return row == lane // LANES


def copies_kernel(source, listed, out, ids, sem):
    copy = pltpu.make_async_copy(listed, ids, sem)
    copy.start()
    for y in range(YN):
        out[y] = source[...]
    copy.wait()


STEP = 4


def list_active(ids, order, which, core, c, found=None):
    count = jnp.int32(0)
    for e in range(ENTRIES):
        tile = ids[c, e // REFS, e % REFS]
        active = (tile >= 0) & (tile % CN == core)
        order[which, count] = e
        if found is not None:
            pl.when(active)(lambda e=e: found(e))
        count = count + active.astype(jnp.int32)
    return count


def over_active(count, footprints, ids, order, which, c, work, ready=None):
    def step(i, carry):
        entries = []
        for u in range(STEP):
            at = i * STEP + u
            real = at < count
            e = order[which, jnp.maximum(jnp.minimum(at, count - 1), 0)]
            if ready is not None:
                pl.when(real)(lambda e=e: ready(e))
            b, k = e // REFS, e % REFS
            entries.append((real, c * BLOCKS + b, ids[c, b, k], footprints.at[b, k]))
        work(entries)
        return carry

    lax.fori_loop(0, (count + STEP - 1) // STEP, step, 0)


def predict_kernel(panels, own, mate, ids, out, held, order, sem, totals):
    core = lax.axis_index("c")

    def copy(e):
        b, k = e // REFS, e % REFS
        return pltpu.make_async_copy(own.at[b, k], held.at[b, k], sem.at[e])

    count = list_active(ids, order, 0, core, core, lambda e: copy(e).start())
    count_mate = list_active(ids, order, 1, core, 1 - core)
    match = diagonal()
    totals[...] = jnp.zeros_like(totals)

    def work(found):
        terms = []
        for real, _, tile, footprint in found:
            panel = panels[tile // CN % YN, tile // (CN * YN)].astype(F32)
            panel = jnp.where(real, panel, 0.0)
            left = jnp.concatenate(
                [jnp.where(match, jnp.concatenate([block(panel, t)] * SUB, axis=1), 0.0) for t in range(TRACERS)],
                axis=0,
            ).astype(BF16)
            terms.append(
                lax.dot_general(left, footprint[...], (((1,), (1,)), ((), ())), preferred_element_type=F32)
            )
        for (_, b, _, _), term in zip(found, terms):
            totals[b] = totals[b] + term

    over_active(count_mate, mate, ids, order, 1, 1 - core, work)
    over_active(count, held, ids, order, 0, core, work, lambda e: copy(e).wait())
    rows = [
        jnp.sum(totals[b, t * SUB : (t + 1) * SUB], axis=0, keepdims=True)
        for t in range(TRACERS)
        for b in range(CN * BLOCKS)
    ]
    whole = jnp.concatenate(rows, axis=0)
    for peer in range(out.shape[0]):
        out[peer] = whole


def adjoint_kernel(parts, both, held, mate, ids, misfits, out, order, lefts, sums):
    core = lax.axis_index("c")
    count = list_active(ids, order, 0, core, core)
    count_mate = list_active(ids, order, 1, core, 1 - core)
    whole = parts[0]
    for peer in range(1, parts.shape[0]):
        whole = whole + parts[peer]

    def seen(which):
        rows = []
        for t in range(TRACERS):
            for c in range(CN):
                for b in range(BLOCKS):
                    r, at = seen_row(which, t, b)
                    rows.append(both[c, r : r + 1, at : at + LANES])
        return jnp.concatenate(rows, axis=0)

    misfit = (whole - seen(0)) * seen(1)
    misfits[...] = misfit
    for b in range(CN * BLOCKS):
        lefts[b] = jnp.concatenate(
            [jnp.broadcast_to(misfit[t * SUB + b : t * SUB + b + 1], (SUB, SIGHTS)) for t in range(TRACERS)], axis=0
        )
    sums[...] = jnp.zeros_like(sums)
    row = lax.broadcasted_iota(jnp.int32, (SUB, LANES), 0)

    def work(found):
        values = []
        for real, b, _, footprint in found:
            full = jnp.dot(lefts[b].astype(BF16), footprint[...], preferred_element_type=F32)
            blocks = []
            for t in range(TRACERS):
                mine = full[t * SUB : (t + 1) * SUB]
                value = block(mine, 0)
                for q in range(1, SUB):
                    value = jnp.where(row == q, block(mine, q), value)
                blocks.append(jnp.where(real, value, 0.0))
            values.append(jnp.concatenate(blocks, axis=1))
        for (_, _, tile, _), value in zip(found, values):
            y, z = tile // CN % YN, tile // (CN * YN)
            sums[y, z] = sums[y, z] + value

    over_active(count, held, ids, order, 0, core, work)
    over_active(count_mate, mate, ids, order, 1, 1 - core, work)
    out[...] = sums[...].astype(BF16)


LEVELS, SPACING = 5, 0.4
FINE = 256.0


def fold_y_kernel(parts, out):
    for z in range(ZN):
        value = parts[0, z].astype(F32)
        for y in range(1, YN):
            value = value + parts[y, z].astype(F32)
        wide = value * 65537.0
        near = wide - (wide - value)
        size = jnp.abs(near)
        part = (value - near) * (FINE / SPACING / jnp.where(size == 0.0, 1.0, size))
        level = jnp.clip(jnp.floor(part + LEVELS / 2), 0.0, LEVELS - 1.0)
        code = block(level, 0) + LEVELS * block(level, 1) + LEVELS * LEVELS * block(level, 2)
        out[z, :, :PAY] = near.astype(BF16)
        out[z, :, PAY:] = code.astype(BF16)


def fold_z_kernel(parts, out):
    total = None
    for z in range(ZN):
        near = parts[z, :, :PAY].astype(F32)
        code = parts[z, :, PAY:].astype(F32)
        third = jnp.floor((code + 0.5) * (1.0 / (LEVELS * LEVELS)))
        code = code - LEVELS * LEVELS * third
        second = jnp.floor((code + 0.5) * (1.0 / LEVELS))
        level = jnp.concatenate([code - LEVELS * second, second, third], axis=1)
        part = (level - LEVELS // 2) * (SPACING / FINE)
        value = near + jnp.abs(near) * part
        total = value if total is None else total + value
    out[...] = total


def final_kernel(total_both, total_other, both, other, misfits, out, residual):
    core, here = lax.axis_index("c"), lax.axis_index(OBS)
    for t in range(TRACERS):
        for b in range(BLOCKS):
            first, second = (misfits[at : at + 1] for at in (t * SUB + b, t * SUB + BLOCKS + b))
            residual[t : t + 1, b * SIGHTS : (b + 1) * SIGHTS] = jnp.where(core == 0, first, second)
    sweeps = Sweeps(around(both, other, core, TRACERS), here)
    for t in range(TRACERS):
        value = both[core, :, t * LANES : (t + 1) * LANES] + sweeps.twice(around(total_both, total_other, core, t))
        for s in range(SUB):
            r, at = s // CHUNKS, s % CHUNKS * LANES
            out[t, 0, r : r + 1, at : at + LANES] = value[s : s + 1]


def neighbours(own, head):
    pairs = [(i, i + 1) for i in range(1, TILES - 1, 2)]
    other = lax.ppermute(head, OBS, pairs + [(b, a) for a, b in pairs])
    return lax.all_gather(own, "c"), other


def run_predict(panels, footprints, mate, ids, peers):
    return call(
        predict_kernel,
        (shape(peers, TRACERS * SUB, LANES), pltpu.VMEM(footprints.shape, BF16)),
        [VMEM, HBM, VMEM, SMEM],
        16,
        [
            pltpu.SMEM((CN, ENTRIES + 1), jnp.int32),
            pltpu.SemaphoreType.DMA((ENTRIES,)),
            pltpu.VMEM((CN * BLOCKS, TRACERS * SUB, LANES), F32),
        ],
        name="predict",
    )(panels, in_hbm(footprints), mate, ids)


def run_adjoint(parts, both, held, mate, ids):
    return call(
        adjoint_kernel,
        (shape(TRACERS * SUB, SIGHTS), shape(YN, ZN, SUB, PAY, dtype=BF16)),
        [VMEM] * 4 + [SMEM],
        16,
        [
            pltpu.SMEM((CN, ENTRIES + 1), jnp.int32),
            pltpu.VMEM((CN * BLOCKS, TRACERS * SUB, LANES), F32),
            pltpu.VMEM((YN, ZN, SUB, PAY), F32),
        ],
        name="adjoint",
    )(parts, both, held, mate, ids)


def shards(control, diffusivity, footprints, tile_lists, tile_counts, measured, weight):
    given = (control, diffusivity, measured, weight, tile_lists, tile_counts.reshape(1, BLOCKS))
    own, head = call(
        pack_kernel,
        (shape(SUB, PACK), shape(SUB, IDS * LANES)),
        [HBM] * len(given),
        1,
        [pltpu.VMEM(a.shape, a.dtype) for a in given] + [pltpu.SemaphoreType.DMA((len(given),))],
        name="pack",
    )(*map(in_hbm, given))
    both, other = neighbours(own, head)
    flux, listed = call(
        flux_kernel,
        (shape(ZN, SUB, PAY, dtype=BF16), shape(CN, BLOCKS, LANES, dtype=jnp.int32)),
        [VMEM] * 2,
        2,
        name="flux",
    )(both, other)

    by_z = lax.all_to_all(flux, "z", 0, 0, tiled=True)
    by_z, footprints = lax.optimization_barrier((by_z, footprints))
    mate = lax.ppermute(footprints, "c", [(0, 1), (1, 0)])
    copies, ids = call(
        copies_kernel,
        (shape(YN, *by_z.shape, dtype=BF16), pltpu.SMEM(listed.shape, jnp.int32)),
        [VMEM] * 2,
        2,
        [pltpu.SemaphoreType.DMA],
        name="copies",
    )(by_z, listed)
    panels = lax.all_to_all(copies, "y", 0, 0, tiled=True)

    part, held = run_predict(panels, footprints, mate, ids, lax.axis_size("tm") * CN)
    parts = lax.all_to_all(part, ("tm", "c"), 0, 0, tiled=True)
    misfits, dense = run_adjoint(parts, both, held, mate, ids)

    over_y = lax.all_to_all(dense, "y", 0, 0, tiled=True)
    coded = call(fold_y_kernel, shape(ZN, SUB, PAY + LANES, dtype=BF16), [VMEM], 2, name="fold_y")(over_y)
    over_z = lax.all_to_all(coded, "z", 0, 0, tiled=True)
    total = call(fold_z_kernel, shape(SUB, PAY), [VMEM], 2, name="fold_z")(over_z)

    total_both, total_other = neighbours(total, total)
    return call(
        final_kernel,
        (shape(*control.shape), shape(TRACERS, BLOCKS * SIGHTS)),
        [VMEM] * 5,
        2,
        name="final",
    )(total_both, total_other, both, other, misfits)


def solution(mesh):
    fine = Mesh(mesh.devices.reshape(mesh.shape["tm"], ZN, YN, CN), ("tm",) + OBS)
    placed = (
        P(None, "tm", OBS, None),
        P(OBS, None),
        P(OBS, None, None, "tm"),
        P(OBS, None),
        P(OBS),
        P(None, OBS),
        P(None, OBS),
    )
    return jax.shard_map(
        shards,
        mesh=fine,
        in_specs=placed,
        out_specs=(P(None, "tm", OBS, None), P(None, OBS)),
        check_vma=False,
    )
```

```python
import jax
import jax.numpy as jnp
from jax import lax
from jax.experimental import pallas as pl
from jax.experimental.pallas import tpu as pltpu
from jax.sharding import Mesh, PartitionSpec as P

ZN, YN, CN = 16, 4, 2
OBS = ("z", "y", "c")
TILES = ZN * YN * CN
TRACERS, ROWS, WIDTH = 3, 2, 512
LANES = 128
CHUNKS = WIDTH // LANES
SUB = ROWS * CHUNKS
CELLS = ROWS * WIDTH
BLOCKS, REFS, SIGHTS = 4, 4, 128
ENTRIES = BLOCKS * REFS
PAY = TRACERS * LANES
F32, BF16 = jnp.float32, jnp.bfloat16


VMEM = pl.BlockSpec(memory_space=pltpu.VMEM)
SMEM = pl.BlockSpec(memory_space=pltpu.SMEM)
HBM = pl.BlockSpec(memory_space=pltpu.HBM)
MIB = 1 << 20


def call(body, out, ins, mib, scratch=(), name=None):
    return pl.pallas_call(
        body,
        out_shape=out,
        in_specs=ins,
        out_specs=jax.tree.map(lambda o: SMEM if getattr(o, "memory_space", None) == pltpu.SMEM else VMEM, out),
        scratch_shapes=list(scratch),
        compiler_params=pltpu.CompilerParams(vmem_limit_bytes=mib * MIB),
        name=name,
    )


def in_hbm(array):
    return pltpu.with_memory_space_constraint(array, pltpu.HBM)


def shape(*dims, dtype=F32):
    return jax.ShapeDtypeStruct(dims, dtype)


def block(value, t):
    return value[:, t * LANES : (t + 1) * LANES]


IDS, SEEN = 4, 5
PACK = 8 * LANES


def seen_row(which, t, b):
    at = (which * TRACERS + t) * BLOCKS + b
    return at % SUB, (SEEN + at // SUB) * LANES


def pack_kernel(*refs):
    sources, (out, head), targets, sem = refs[:6], refs[6:8], refs[8:14], refs[14]
    copies = [pltpu.make_async_copy(a, b, sem.at[i]) for i, (a, b) in enumerate(zip(sources, targets))]
    for copy in copies:
        copy.start()
    for copy in copies:
        copy.wait()
    control, diffusivity, measured, weight, lists, counts = targets

    def rows(read):
        return jnp.concatenate([read(s // CHUNKS, s % CHUNKS * LANES) for s in range(SUB)], axis=0)

    for t in range(TRACERS):
        head[:, t * LANES : (t + 1) * LANES] = rows(lambda r, at, t=t: control[t, 0, r : r + 1, at : at + LANES])
    head[:, TRACERS * LANES :] = rows(lambda r, at: diffusivity[r : r + 1, at : at + LANES])
    out[:, : IDS * LANES] = head[...]
    lane = lax.broadcasted_iota(jnp.int32, (BLOCKS, REFS), 1)
    row = lax.broadcasted_iota(jnp.int32, (BLOCKS, REFS), 0)
    limit = jnp.zeros((BLOCKS, REFS), jnp.int32)
    for b in range(BLOCKS):
        limit = jnp.where(row == b, counts[0:1, b : b + 1], limit)
    out[:BLOCKS, IDS * LANES : IDS * LANES + REFS] = jnp.where(lane < limit, lists[...], -1).astype(F32)
    for which, ref in enumerate((measured, weight)):
        for t in range(TRACERS):
            for b in range(BLOCKS):
                r, at = seen_row(which, t, b)
                out[r : r + 1, at : at + LANES] = ref[t : t + 1, b * SIGHTS : (b + 1) * SIGHTS]


def around(both, other, core, t):
    own = both[core, :, t * LANES : (t + 1) * LANES]
    mate = both[1 - core, :, t * LANES : (t + 1) * LANES]
    far = other[:, t * LANES : (t + 1) * LANES]
    first = core == 0
    return jnp.concatenate([jnp.where(first, far, mate), own, jnp.where(first, mate, far)], axis=0)


class Sweeps:
    def __init__(self, conduct, here):
        whole = conduct.shape
        self.rows = whole[0]
        sub = lax.broadcasted_iota(jnp.int32, whole, 0)
        self.lane = lax.broadcasted_iota(jnp.int32, whole, 1)
        self.chunk = sub % CHUNKS
        grid_row = sub // CHUNKS - ROWS
        self.inside = ((grid_row >= 0) | (here > 0)) & ((grid_row < ROWS) | (here < TILES - 1))
        self.factors = [0.0625 * (conduct + nb) for nb in self.neighbours(conduct)]

    def neighbours(self, v):
        n = self.rows
        up = pltpu.roll(v, CHUNKS, 0)
        down = pltpu.roll(v, n - CHUNKS, 0)
        left = pltpu.roll(v, 1, 1)
        left = jnp.where(self.lane == 0, jnp.where(self.chunk == 0, 0.0, pltpu.roll(left, 1, 0)), left)
        right = pltpu.roll(v, LANES - 1, 1)
        right = jnp.where(
            self.lane == LANES - 1, jnp.where(self.chunk == CHUNKS - 1, 0.0, pltpu.roll(right, n - 1, 0)), right
        )
        return up, down, left, right

    def once(self, v):
        total = v
        for factor, nb in zip(self.factors, self.neighbours(v)):
            total = total + factor * (nb - v)
        return total

    def twice(self, v):
        return self.once(jnp.where(self.inside, self.once(v), 0.0))[SUB : 2 * SUB]


def flux_kernel(both, other, out):
    core, here = lax.axis_index("c"), lax.axis_index(OBS)
    sweeps = Sweeps(around(both, other, core, TRACERS), here)
    half = jnp.concatenate([sweeps.twice(around(both, other, core, t)) for t in range(TRACERS)], axis=1).astype(BF16)
    for z in range(ZN):
        out[z] = half


def diagonal():
    row = lax.broadcasted_iota(jnp.int32, (SUB, CELLS), 0)
    lane = lax.broadcasted_iota(jnp.int32, (SUB, CELLS), 1)
    return row == lane // LANES


def copies_kernel(source, out):
    for y in range(YN):
        out[y] = source[...]


def lists_kernel(both, ids, order, numbers, sem):
    core = lax.axis_index("c")
    for c in range(CN):
        numbers[c] = both[c, :BLOCKS, IDS * LANES : SEEN * LANES].astype(jnp.int32)
    copy = pltpu.make_async_copy(numbers, ids, sem)
    copy.start()
    copy.wait()
    for which, c in ((0, core), (1, 1 - core)):
        count = jnp.int32(0)
        for e in range(ENTRIES):
            tile = ids[c, e // REFS, e % REFS]
            order[which, count] = e
            count = count + ((tile >= 0) & (tile % CN == core)).astype(jnp.int32)
        order[which, ENTRIES] = count


STEP = 4


def over_active(footprints, ids, order, which, c, work, ready=None):
    count = order[which, ENTRIES]

    def step(i, carry):
        entries = []
        for u in range(STEP):
            at = i * STEP + u
            real = at < count
            e = order[which, jnp.maximum(jnp.minimum(at, count - 1), 0)]
            if ready is not None:
                pl.when(real)(lambda e=e: ready(e))
            b, k = e // REFS, e % REFS
            entries.append((real, c * BLOCKS + b, ids[c, b, k], footprints.at[b, k]))
        work(entries)
        return carry

    lax.fori_loop(0, (count + STEP - 1) // STEP, step, 0)


def predict_kernel(panels, own, mate, ids, order, out, held, sem, totals):
    core = lax.axis_index("c")

    def copy(e):
        b, k = e // REFS, e % REFS
        return pltpu.make_async_copy(own.at[b, k], held.at[b, k], sem.at[e])

    def start(i, carry):
        copy(order[0, i]).start()
        return carry

    lax.fori_loop(0, order[0, ENTRIES], start, 0)
    match = diagonal()
    totals[...] = jnp.zeros_like(totals)

    def work(found):
        terms = []
        for real, _, tile, footprint in found:
            panel = panels[tile // CN % YN, tile // (CN * YN)].astype(F32)
            panel = jnp.where(real, panel, 0.0)
            left = jnp.concatenate(
                [jnp.where(match, jnp.concatenate([block(panel, t)] * SUB, axis=1), 0.0) for t in range(TRACERS)],
                axis=0,
            ).astype(BF16)
            terms.append(
                lax.dot_general(left, footprint[...], (((1,), (1,)), ((), ())), preferred_element_type=F32)
            )
        for (_, b, _, _), term in zip(found, terms):
            totals[b] = totals[b] + term

    over_active(mate, ids, order, 1, 1 - core, work)
    over_active(held, ids, order, 0, core, work, lambda e: copy(e).wait())
    rows = [
        jnp.sum(totals[b, t * SUB : (t + 1) * SUB], axis=0, keepdims=True)
        for t in range(TRACERS)
        for b in range(CN * BLOCKS)
    ]
    whole = jnp.concatenate(rows, axis=0)
    for peer in range(out.shape[0]):
        out[peer] = whole


def adjoint_kernel(parts, both, held, mate, ids, order, misfits, out, lefts, sums):
    core = lax.axis_index("c")
    whole = parts[0]
    for peer in range(1, parts.shape[0]):
        whole = whole + parts[peer]

    def seen(which):
        rows = []
        for t in range(TRACERS):
            for c in range(CN):
                for b in range(BLOCKS):
                    r, at = seen_row(which, t, b)
                    rows.append(both[c, r : r + 1, at : at + LANES])
        return jnp.concatenate(rows, axis=0)

    misfit = (whole - seen(0)) * seen(1)
    misfits[...] = misfit
    for b in range(CN * BLOCKS):
        lefts[b] = jnp.concatenate(
            [jnp.broadcast_to(misfit[t * SUB + b : t * SUB + b + 1], (SUB, SIGHTS)) for t in range(TRACERS)], axis=0
        )
    sums[...] = jnp.zeros_like(sums)
    row = lax.broadcasted_iota(jnp.int32, (SUB, LANES), 0)

    def work(found):
        values = []
        for real, b, _, footprint in found:
            full = jnp.dot(lefts[b].astype(BF16), footprint[...], preferred_element_type=F32)
            blocks = []
            for t in range(TRACERS):
                mine = full[t * SUB : (t + 1) * SUB]
                value = block(mine, 0)
                for q in range(1, SUB):
                    value = jnp.where(row == q, block(mine, q), value)
                blocks.append(jnp.where(real, value, 0.0))
            values.append(jnp.concatenate(blocks, axis=1))
        for (_, _, tile, _), value in zip(found, values):
            y, z = tile // CN % YN, tile // (CN * YN)
            sums[y, z] = sums[y, z] + value

    over_active(held, ids, order, 0, core, work)
    over_active(mate, ids, order, 1, 1 - core, work)
    out[...] = sums[...].astype(BF16)


LEVELS, SPACING = 5, 0.4
FINE = 256.0


def fold_y_kernel(parts, out):
    for z in range(ZN):
        value = parts[0, z].astype(F32)
        for y in range(1, YN):
            value = value + parts[y, z].astype(F32)
        wide = value * 65537.0
        near = wide - (wide - value)
        size = jnp.abs(near)
        part = (value - near) * (FINE / SPACING / jnp.where(size == 0.0, 1.0, size))
        level = jnp.clip(jnp.floor(part + LEVELS / 2), 0.0, LEVELS - 1.0)
        code = block(level, 0) + LEVELS * block(level, 1) + LEVELS * LEVELS * block(level, 2)
        out[z, :, :PAY] = near.astype(BF16)
        out[z, :, PAY:] = code.astype(BF16)


def fold_z_kernel(parts, out):
    total = None
    for z in range(ZN):
        near = parts[z, :, :PAY].astype(F32)
        code = parts[z, :, PAY:].astype(F32)
        third = jnp.floor((code + 0.5) * (1.0 / (LEVELS * LEVELS)))
        code = code - LEVELS * LEVELS * third
        second = jnp.floor((code + 0.5) * (1.0 / LEVELS))
        level = jnp.concatenate([code - LEVELS * second, second, third], axis=1)
        part = (level - LEVELS // 2) * (SPACING / FINE)
        value = near + jnp.abs(near) * part
        total = value if total is None else total + value
    out[...] = total


def final_kernel(total_both, total_other, both, other, misfits, out, residual):
    core, here = lax.axis_index("c"), lax.axis_index(OBS)
    for t in range(TRACERS):
        for b in range(BLOCKS):
            first, second = (misfits[at : at + 1] for at in (t * SUB + b, t * SUB + BLOCKS + b))
            residual[t : t + 1, b * SIGHTS : (b + 1) * SIGHTS] = jnp.where(core == 0, first, second)
    sweeps = Sweeps(around(both, other, core, TRACERS), here)
    for t in range(TRACERS):
        value = both[core, :, t * LANES : (t + 1) * LANES] + sweeps.twice(around(total_both, total_other, core, t))
        for s in range(SUB):
            r, at = s // CHUNKS, s % CHUNKS * LANES
            out[t, 0, r : r + 1, at : at + LANES] = value[s : s + 1]


def neighbours(own, head):
    pairs = [(i, i + 1) for i in range(1, TILES - 1, 2)]
    other = lax.ppermute(head, OBS, pairs + [(b, a) for a, b in pairs])
    return lax.all_gather(own, "c"), other


def run_predict(panels, footprints, mate, ids, order, peers):
    return call(
        predict_kernel,
        (shape(peers, TRACERS * SUB, LANES), pltpu.VMEM(footprints.shape, BF16)),
        [VMEM, HBM, VMEM, SMEM, SMEM],
        16,
        [
            pltpu.SemaphoreType.DMA((ENTRIES,)),
            pltpu.VMEM((CN * BLOCKS, TRACERS * SUB, LANES), F32),
        ],
        name="predict",
    )(panels, in_hbm(footprints), mate, ids, order)


def run_adjoint(parts, both, held, mate, ids, order):
    return call(
        adjoint_kernel,
        (shape(TRACERS * SUB, SIGHTS), shape(YN, ZN, SUB, PAY, dtype=BF16)),
        [VMEM] * 4 + [SMEM] * 2,
        16,
        [
            pltpu.VMEM((CN * BLOCKS, TRACERS * SUB, LANES), F32),
            pltpu.VMEM((YN, ZN, SUB, PAY), F32),
        ],
        name="adjoint",
    )(parts, both, held, mate, ids, order)


def shards(control, diffusivity, footprints, tile_lists, tile_counts, measured, weight):
    given = (control, diffusivity, measured, weight, tile_lists, tile_counts.reshape(1, BLOCKS))
    own, head = call(
        pack_kernel,
        (shape(SUB, PACK), shape(SUB, IDS * LANES)),
        [HBM] * len(given),
        1,
        [pltpu.VMEM(a.shape, a.dtype) for a in given] + [pltpu.SemaphoreType.DMA((len(given),))],
        name="pack",
    )(*map(in_hbm, given))
    both, other = neighbours(own, head)
    ids, order = call(
        lists_kernel,
        (pltpu.SMEM((CN, BLOCKS, LANES), jnp.int32), pltpu.SMEM((CN, ENTRIES + 1), jnp.int32)),
        [VMEM],
        1,
        [pltpu.VMEM((CN, BLOCKS, LANES), jnp.int32), pltpu.SemaphoreType.DMA],
        name="lists",
    )(both)
    both, ids, order = lax.optimization_barrier((both, ids, order))
    flux = call(flux_kernel, shape(ZN, SUB, PAY, dtype=BF16), [VMEM] * 2, 2, name="flux")(both, other)

    by_z = lax.all_to_all(flux, "z", 0, 0, tiled=True)
    by_z, footprints = lax.optimization_barrier((by_z, footprints))
    mate = lax.ppermute(footprints, "c", [(0, 1), (1, 0)])
    copies = call(copies_kernel, shape(YN, *by_z.shape, dtype=BF16), [VMEM], 2, name="copies")(by_z)
    panels = lax.all_to_all(copies, "y", 0, 0, tiled=True)

    part, held = run_predict(panels, footprints, mate, ids, order, lax.axis_size("tm") * CN)
    parts = lax.all_to_all(part, ("tm", "c"), 0, 0, tiled=True)
    misfits, dense = run_adjoint(parts, both, held, mate, ids, order)

    over_y = lax.all_to_all(dense, "y", 0, 0, tiled=True)
    coded = call(fold_y_kernel, shape(ZN, SUB, PAY + LANES, dtype=BF16), [VMEM], 2, name="fold_y")(over_y)
    over_z = lax.all_to_all(coded, "z", 0, 0, tiled=True)
    total = call(fold_z_kernel, shape(SUB, PAY), [VMEM], 2, name="fold_z")(over_z)

    total_both, total_other = neighbours(total, total)
    return call(
        final_kernel,
        (shape(*control.shape), shape(TRACERS, BLOCKS * SIGHTS)),
        [VMEM] * 5,
        2,
        name="final",
    )(total_both, total_other, both, other, misfits)


def solution(mesh):
    fine = Mesh(mesh.devices.reshape(mesh.shape["tm"], ZN, YN, CN), ("tm",) + OBS)
    placed = (
        P(None, "tm", OBS, None),
        P(OBS, None),
        P(OBS, None, None, "tm"),
        P(OBS, None),
        P(OBS),
        P(None, OBS),
        P(None, OBS),
    )
    return jax.shard_map(
        shards,
        mesh=fine,
        in_specs=placed,
        out_specs=(P(None, "tm", OBS, None), P(None, OBS)),
        check_vma=False,
    )
```

```python
import jax
import jax.numpy as jnp
from jax import lax
from jax.experimental import pallas as pl
from jax.experimental.pallas import tpu as pltpu
from jax.sharding import Mesh, PartitionSpec as P

ZN, YN, CN = 16, 4, 2
OBS = ("z", "y", "c")
TILES = ZN * YN * CN
TRACERS, ROWS, WIDTH = 3, 2, 512
LANES = 128
CHUNKS = WIDTH // LANES
SUB = ROWS * CHUNKS
CELLS = ROWS * WIDTH
BLOCKS, REFS, SIGHTS = 4, 4, 128
ENTRIES = BLOCKS * REFS
PAY = TRACERS * LANES
F32, BF16 = jnp.float32, jnp.bfloat16


VMEM = pl.BlockSpec(memory_space=pltpu.VMEM)
SMEM = pl.BlockSpec(memory_space=pltpu.SMEM)
HBM = pl.BlockSpec(memory_space=pltpu.HBM)
MIB = 1 << 20


def call(body, out, ins, mib, scratch=(), name=None):
    return pl.pallas_call(
        body,
        out_shape=out,
        in_specs=ins,
        out_specs=jax.tree.map(lambda o: SMEM if getattr(o, "memory_space", None) == pltpu.SMEM else VMEM, out),
        scratch_shapes=list(scratch),
        compiler_params=pltpu.CompilerParams(vmem_limit_bytes=mib * MIB),
        name=name,
    )


def in_hbm(array):
    return pltpu.with_memory_space_constraint(array, pltpu.HBM)


def shape(*dims, dtype=F32):
    return jax.ShapeDtypeStruct(dims, dtype)


def block(value, t):
    return value[:, t * LANES : (t + 1) * LANES]


IDS, SEEN = 4, 5
PACK = 8 * LANES


def seen_row(which, t, b):
    at = (which * TRACERS + t) * BLOCKS + b
    return at % SUB, (SEEN + at // SUB) * LANES


def pack_kernel(*refs):
    sources, (out, head), targets, sem = refs[:6], refs[6:8], refs[8:14], refs[14]
    copies = [pltpu.make_async_copy(a, b, sem.at[i]) for i, (a, b) in enumerate(zip(sources, targets))]
    for copy in copies:
        copy.start()
    for copy in copies:
        copy.wait()
    control, diffusivity, measured, weight, lists, counts = targets

    def rows(read):
        return jnp.concatenate([read(s // CHUNKS, s % CHUNKS * LANES) for s in range(SUB)], axis=0)

    for t in range(TRACERS):
        head[:, t * LANES : (t + 1) * LANES] = rows(lambda r, at, t=t: control[t, 0, r : r + 1, at : at + LANES])
    head[:, TRACERS * LANES :] = rows(lambda r, at: diffusivity[r : r + 1, at : at + LANES])
    out[:, : IDS * LANES] = head[...]
    lane = lax.broadcasted_iota(jnp.int32, (BLOCKS, REFS), 1)
    row = lax.broadcasted_iota(jnp.int32, (BLOCKS, REFS), 0)
    limit = jnp.zeros((BLOCKS, REFS), jnp.int32)
    for b in range(BLOCKS):
        limit = jnp.where(row == b, counts[0:1, b : b + 1], limit)
    out[:, IDS * LANES : SEEN * LANES] = jnp.zeros((SUB, LANES), F32)
    out[:BLOCKS, IDS * LANES : IDS * LANES + REFS] = jnp.where(lane < limit, lists[...], -1).astype(F32)
    for which, ref in enumerate((measured, weight)):
        for t in range(TRACERS):
            for b in range(BLOCKS):
                r, at = seen_row(which, t, b)
                out[r : r + 1, at : at + LANES] = ref[t : t + 1, b * SIGHTS : (b + 1) * SIGHTS]


def around(both, other, core, t):
    own = both[core, :, t * LANES : (t + 1) * LANES]
    mate = both[1 - core, :, t * LANES : (t + 1) * LANES]
    far = other[:, t * LANES : (t + 1) * LANES]
    first = core == 0
    return jnp.concatenate([jnp.where(first, far, mate), own, jnp.where(first, mate, far)], axis=0)


class Sweeps:
    def __init__(self, conduct, here):
        whole = conduct.shape
        self.rows = whole[0]
        sub = lax.broadcasted_iota(jnp.int32, whole, 0)
        self.lane = lax.broadcasted_iota(jnp.int32, whole, 1)
        self.chunk = sub % CHUNKS
        grid_row = sub // CHUNKS - ROWS
        self.inside = ((grid_row >= 0) | (here > 0)) & ((grid_row < ROWS) | (here < TILES - 1))
        self.factors = [0.0625 * (conduct + nb) for nb in self.neighbours(conduct)]

    def neighbours(self, v):
        n = self.rows
        up = pltpu.roll(v, CHUNKS, 0)
        down = pltpu.roll(v, n - CHUNKS, 0)
        left = pltpu.roll(v, 1, 1)
        left = jnp.where(self.lane == 0, jnp.where(self.chunk == 0, 0.0, pltpu.roll(left, 1, 0)), left)
        right = pltpu.roll(v, LANES - 1, 1)
        right = jnp.where(
            self.lane == LANES - 1, jnp.where(self.chunk == CHUNKS - 1, 0.0, pltpu.roll(right, n - 1, 0)), right
        )
        return up, down, left, right

    def once(self, v):
        total = v
        for factor, nb in zip(self.factors, self.neighbours(v)):
            total = total + factor * (nb - v)
        return total

    def twice(self, v):
        return self.once(jnp.where(self.inside, self.once(v), 0.0))[SUB : 2 * SUB]


def flux_kernel(both, other, out):
    core, here = lax.axis_index("c"), lax.axis_index(OBS)
    sweeps = Sweeps(around(both, other, core, TRACERS), here)
    half = jnp.concatenate([sweeps.twice(around(both, other, core, t)) for t in range(TRACERS)], axis=1).astype(BF16)
    for z in range(ZN):
        out[z] = half


def diagonal():
    row = lax.broadcasted_iota(jnp.int32, (SUB, CELLS), 0)
    lane = lax.broadcasted_iota(jnp.int32, (SUB, CELLS), 1)
    return row == lane // LANES


def copies_kernel(source, out):
    for y in range(YN):
        out[y] = source[...]


def lists_kernel(both, ids, order, numbers, sem):
    core = lax.axis_index("c")
    for c in range(CN):
        numbers[c] = both[c, :BLOCKS, IDS * LANES : SEEN * LANES].astype(jnp.int32)
    copy = pltpu.make_async_copy(numbers, ids, sem)
    copy.start()
    copy.wait()
    for which, c in ((0, core), (1, 1 - core)):
        count = jnp.int32(0)
        for e in range(ENTRIES):
            tile = ids[c, e // REFS, e % REFS]
            order[which, count] = e
            count = count + ((tile >= 0) & (tile % CN == core)).astype(jnp.int32)
        order[which, ENTRIES] = count


STEP = 4


def over_active(footprints, ids, order, which, c, work, ready=None):
    count = order[which, ENTRIES]

    def step(i, carry):
        entries = []
        for u in range(STEP):
            at = i * STEP + u
            real = at < count
            e = order[which, jnp.maximum(jnp.minimum(at, count - 1), 0)]
            if ready is not None:
                pl.when(real)(lambda e=e: ready(e))
            b, k = e // REFS, e % REFS
            entries.append((real, c * BLOCKS + b, ids[c, b, k], footprints.at[b, k]))
        work(entries)
        return carry

    lax.fori_loop(0, (count + STEP - 1) // STEP, step, 0)


def predict_kernel(panels, own, mate, ids, order, out, held, sem, totals):
    core = lax.axis_index("c")

    def copy(e):
        b, k = e // REFS, e % REFS
        return pltpu.make_async_copy(own.at[b, k], held.at[b, k], sem.at[e])

    def start(i, carry):
        copy(order[0, i]).start()
        return carry

    lax.fori_loop(0, order[0, ENTRIES], start, 0)
    match = diagonal()
    totals[...] = jnp.zeros_like(totals)

    def work(found):
        terms = []
        for real, _, tile, footprint in found:
            panel = panels[tile // CN % YN, tile // (CN * YN)].astype(F32)
            panel = jnp.where(real, panel, 0.0)
            left = jnp.concatenate(
                [jnp.where(match, jnp.concatenate([block(panel, t)] * SUB, axis=1), 0.0) for t in range(TRACERS)],
                axis=0,
            ).astype(BF16)
            terms.append(
                lax.dot_general(left, footprint[...], (((1,), (1,)), ((), ())), preferred_element_type=F32)
            )
        for (_, b, _, _), term in zip(found, terms):
            totals[b] = totals[b] + term

    over_active(mate, ids, order, 1, 1 - core, work)
    over_active(held, ids, order, 0, core, work, lambda e: copy(e).wait())
    rows = [
        jnp.sum(totals[b, t * SUB : (t + 1) * SUB], axis=0, keepdims=True)
        for t in range(TRACERS)
        for b in range(CN * BLOCKS)
    ]
    whole = jnp.concatenate(rows, axis=0)
    for peer in range(out.shape[0]):
        out[peer] = whole


def adjoint_kernel(parts, both, held, mate, ids, order, misfits, out, lefts, sums):
    core = lax.axis_index("c")
    whole = parts[0]
    for peer in range(1, parts.shape[0]):
        whole = whole + parts[peer]

    def seen(which):
        rows = []
        for t in range(TRACERS):
            for c in range(CN):
                for b in range(BLOCKS):
                    r, at = seen_row(which, t, b)
                    rows.append(both[c, r : r + 1, at : at + LANES])
        return jnp.concatenate(rows, axis=0)

    misfit = (whole - seen(0)) * seen(1)
    misfits[...] = misfit
    for b in range(CN * BLOCKS):
        lefts[b] = jnp.concatenate(
            [jnp.broadcast_to(misfit[t * SUB + b : t * SUB + b + 1], (SUB, SIGHTS)) for t in range(TRACERS)], axis=0
        )
    sums[...] = jnp.zeros_like(sums)
    row = lax.broadcasted_iota(jnp.int32, (SUB, LANES), 0)

    def work(found):
        values = []
        for real, b, _, footprint in found:
            full = jnp.dot(lefts[b].astype(BF16), footprint[...], preferred_element_type=F32)
            blocks = []
            for t in range(TRACERS):
                mine = full[t * SUB : (t + 1) * SUB]
                value = block(mine, 0)
                for q in range(1, SUB):
                    value = jnp.where(row == q, block(mine, q), value)
                blocks.append(jnp.where(real, value, 0.0))
            values.append(jnp.concatenate(blocks, axis=1))
        for (_, _, tile, _), value in zip(found, values):
            y, z = tile // CN % YN, tile // (CN * YN)
            sums[y, z] = sums[y, z] + value

    over_active(held, ids, order, 0, core, work)
    over_active(mate, ids, order, 1, 1 - core, work)
    out[...] = sums[...].astype(BF16)


LEVELS, SPACING = 5, 0.4
FINE = 256.0


def fold_y_kernel(parts, out):
    for z in range(ZN):
        value = parts[0, z].astype(F32)
        for y in range(1, YN):
            value = value + parts[y, z].astype(F32)
        wide = value * 65537.0
        near = wide - (wide - value)
        size = jnp.abs(near)
        part = (value - near) * (FINE / SPACING / jnp.where(size == 0.0, 1.0, size))
        level = jnp.clip(jnp.floor(part + LEVELS / 2), 0.0, LEVELS - 1.0)
        code = block(level, 0) + LEVELS * block(level, 1) + LEVELS * LEVELS * block(level, 2)
        out[z, :, :PAY] = near.astype(BF16)
        out[z, :, PAY:] = code.astype(BF16)


def fold_z_kernel(parts, out):
    total = None
    for z in range(ZN):
        near = parts[z, :, :PAY].astype(F32)
        code = parts[z, :, PAY:].astype(F32)
        third = jnp.floor((code + 0.5) * (1.0 / (LEVELS * LEVELS)))
        code = code - LEVELS * LEVELS * third
        second = jnp.floor((code + 0.5) * (1.0 / LEVELS))
        level = jnp.concatenate([code - LEVELS * second, second, third], axis=1)
        part = (level - LEVELS // 2) * (SPACING / FINE)
        value = near + jnp.abs(near) * part
        total = value if total is None else total + value
    out[...] = total


def final_kernel(total_both, total_other, both, other, misfits, out, residual):
    core, here = lax.axis_index("c"), lax.axis_index(OBS)
    for t in range(TRACERS):
        for b in range(BLOCKS):
            first, second = (misfits[at : at + 1] for at in (t * SUB + b, t * SUB + BLOCKS + b))
            residual[t : t + 1, b * SIGHTS : (b + 1) * SIGHTS] = jnp.where(core == 0, first, second)
    sweeps = Sweeps(around(both, other, core, TRACERS), here)
    for t in range(TRACERS):
        value = both[core, :, t * LANES : (t + 1) * LANES] + sweeps.twice(around(total_both, total_other, core, t))
        for s in range(SUB):
            r, at = s // CHUNKS, s % CHUNKS * LANES
            out[t, 0, r : r + 1, at : at + LANES] = value[s : s + 1]


def neighbours(own, head):
    pairs = [(i, i + 1) for i in range(1, TILES - 1, 2)]
    other = lax.ppermute(head, OBS, pairs + [(b, a) for a, b in pairs])
    return lax.all_gather(own, "c"), other


def run_predict(panels, footprints, mate, ids, order, peers):
    return call(
        predict_kernel,
        (shape(peers, TRACERS * SUB, LANES), pltpu.VMEM(footprints.shape, BF16)),
        [VMEM, HBM, VMEM, SMEM, SMEM],
        16,
        [
            pltpu.SemaphoreType.DMA((ENTRIES,)),
            pltpu.VMEM((CN * BLOCKS, TRACERS * SUB, LANES), F32),
        ],
        name="predict",
    )(panels, in_hbm(footprints), mate, ids, order)


def run_adjoint(parts, both, held, mate, ids, order):
    return call(
        adjoint_kernel,
        (shape(TRACERS * SUB, SIGHTS), shape(YN, ZN, SUB, PAY, dtype=BF16)),
        [VMEM] * 4 + [SMEM] * 2,
        16,
        [
            pltpu.VMEM((CN * BLOCKS, TRACERS * SUB, LANES), F32),
            pltpu.VMEM((YN, ZN, SUB, PAY), F32),
        ],
        name="adjoint",
    )(parts, both, held, mate, ids, order)


def shards(control, diffusivity, footprints, tile_lists, tile_counts, measured, weight):
    given = (control, diffusivity, measured, weight, tile_lists, tile_counts.reshape(1, BLOCKS))
    own, head = call(
        pack_kernel,
        (shape(SUB, PACK), shape(SUB, IDS * LANES)),
        [HBM] * len(given),
        1,
        [pltpu.VMEM(a.shape, a.dtype) for a in given] + [pltpu.SemaphoreType.DMA((len(given),))],
        name="pack",
    )(*map(in_hbm, given))
    both, other = neighbours(own, head)
    ids, order = call(
        lists_kernel,
        (pltpu.SMEM((CN, BLOCKS, LANES), jnp.int32), pltpu.SMEM((CN, ENTRIES + 1), jnp.int32)),
        [VMEM],
        1,
        [pltpu.VMEM((CN, BLOCKS, LANES), jnp.int32), pltpu.SemaphoreType.DMA],
        name="lists",
    )(both)
    both, ids, order = lax.optimization_barrier((both, ids, order))
    flux = call(flux_kernel, shape(ZN, SUB, PAY, dtype=BF16), [VMEM] * 2, 2, name="flux")(both, other)

    by_z = lax.all_to_all(flux, "z", 0, 0, tiled=True)
    by_z, footprints = lax.optimization_barrier((by_z, footprints))
    mate = lax.ppermute(footprints, "c", [(0, 1), (1, 0)])
    copies = call(copies_kernel, shape(YN, *by_z.shape, dtype=BF16), [VMEM], 2, name="copies")(by_z)
    panels = lax.all_to_all(copies, "y", 0, 0, tiled=True)

    part, held = run_predict(panels, footprints, mate, ids, order, lax.axis_size("tm") * CN)
    parts = lax.all_to_all(part, ("tm", "c"), 0, 0, tiled=True)
    misfits, dense = run_adjoint(parts, both, held, mate, ids, order)

    over_y = lax.all_to_all(dense, "y", 0, 0, tiled=True)
    coded = call(fold_y_kernel, shape(ZN, SUB, PAY + LANES, dtype=BF16), [VMEM], 2, name="fold_y")(over_y)
    over_z = lax.all_to_all(coded, "z", 0, 0, tiled=True)
    total = call(fold_z_kernel, shape(SUB, PAY), [VMEM], 2, name="fold_z")(over_z)

    total_both, total_other = neighbours(total, total)
    return call(
        final_kernel,
        (shape(*control.shape), shape(TRACERS, BLOCKS * SIGHTS)),
        [VMEM] * 5,
        2,
        name="final",
    )(total_both, total_other, both, other, misfits)


def solution(mesh):
    fine = Mesh(mesh.devices.reshape(mesh.shape["tm"], ZN, YN, CN), ("tm",) + OBS)
    placed = (
        P(None, "tm", OBS, None),
        P(OBS, None),
        P(OBS, None, None, "tm"),
        P(OBS, None),
        P(OBS),
        P(None, OBS),
        P(None, OBS),
    )
    return jax.shard_map(
        shards,
        mesh=fine,
        in_specs=placed,
        out_specs=(P(None, "tm", OBS, None), P(None, OBS)),
        check_vma=False,
    )
```
